1024 devices in a mesh: node: 64 (over z, y), grp: 16 (over x, core).
Axes of the slice: x: 8, y: 8, z: 8, core: 2. Of those that a mesh axis runs over, the one named last changes fastest.
Arguments:
- nbr_feats: float32 [524288, 512], P(('node', 'grp')), may hold values from -6 to 6
- tgt_feats: float32 [131072, 512], P(('node', 'grp')), may hold values from -6 to 6
- msg_weight: bfloat16 [512, 512], replicated, may hold values from -0.25 to 0.25
- comb_weight: bfloat16 [1024, 512], replicated, may hold values from -0.1875 to 0.1875
- head_gain: float32 [8, 512], replicated, may hold values from 0.3 to 600, as said below
- owners: int32 [131072, 8], P(('node', 'grp')), may hold values from 0 to 63, all different within a row; in each aligned block of 128 rows (0 to 127, 128 to 255, ...) at most 24 rows name the same one
- serve_rows: int32 [1024, 64, 24], P(('node', 'grp')), may hold values from 0 to 511
- importance: int32 [131072, 8], P(('node', 'grp')), may hold values from 1 to 32
- labels: int32 [131072], P('node'), may hold values from 0 to 7
- positives: int32 [131072], P('node'), may hold values from 0 to 2047
Outputs:
- loss: float32 [131072], P(('node', 'grp'))
- grad_msg: float32 [512, 512], P(None, 'grp')
- grad_comb: float32 [1024, 512], P(None, 'grp')
- grad_head: float32 [8, 512], P(None, 'grp')
The draws below stay inside these ranges and needn't reach their ends.
Inputs may be any that keep to these rules, and one draw needn't show every extreme that they name: `owners`: the 8 entries of one target differ. Among the 128 targets of one device no node index is named by more than 24 targets, and some node index is named by exactly 24 targets of some device. `head_gain`: Positive.
All inputs are finite; a program needn't handle non-finite values.
Results may differ from the reference program's by a relative error of at most 0.018.
The reference program's roundings to bfloat16 on the way (of `messages`, `comb_in`, `embed`, `query`, `score_grad`, `pre_grad`, `msg_grad` and `msg_pre_grad`) count: a program that leaves them out, or rounds other values in their place, can miss the bound.
Values may be sent and summed in bfloat16 or wider, within the bound.
A program may use at most 64 MiB of HBM per device.

```python
import math
import jax
import jax.numpy as jnp
import numpy as np
from jax import lax

F = 512
TASKS = 8
NBR = 8
TGT_DEV = 128
ROWS_DEV = 512
CAP = 24
TARGETS = 131072
GROUPT = 2048
NEIGHBOURS = 524288
N_NODE = 64
N_GRP = 16
DEVICES = 1024


def draw_head_gain(key, part):
    key = jax.random.fold_in(key, 7)
    level_key, spread_key = jax.random.split(key)
    level = jnp.exp(jax.random.uniform(level_key, (TASKS, 1), jnp.float32, math.log(0.6), math.log(4.0)))
    spread = jax.random.uniform(spread_key, (TASKS, F), jnp.float32, 0.5, 1.5)
    return level * spread


def touch_ends(entries, rng, least, high):
    place = [jax.random.randint(jax.random.fold_in(rng, axis), (), 0, length) for axis, length in enumerate(entries.shape)]
    longest = entries.shape.index(max(entries.shape))
    beside = place[:longest] + [(place[longest] + 1) % entries.shape[longest]] + place[longest + 1:]
    return entries.at[tuple(place)].set(least).at[tuple(beside)].set(high)


def shard_levels(own_key, dims, pieces, least, high):
    loudness = 1.0
    for dim, blocks in pieces:
        heights = jax.random.uniform(jax.random.fold_in(jax.random.fold_in(own_key, 6), dim), (blocks,), jnp.float32, least / len(pieces), high / len(pieces))
        loudness = loudness * jnp.repeat(jnp.exp(heights), dims[dim] // blocks).reshape((-1,) + (1,) * (len(dims) - 1 - dim))
    return loudness


def deal_out(key, own, number, rows, count, top, most, skew):
    order = jax.random.permutation(key, count)
    crowded, common = load_shares(count, rows * top, most, skew, True), load_shares(count, rows * top, most, skew, False)
    places = jnp.arange(count)

    def named(tallies, offset_by):
        used = int((tallies > 0).sum())
        fixed = max(1, used // 4)
        moved = fixed + (places - fixed + offset_by * (used - fixed)) % max(1, count - fixed)
        return jnp.zeros((count,), jnp.int32).at[order[jnp.where(places < fixed, places, moved)]].set(jnp.asarray(tallies, jnp.int32))

    tallies = jnp.where(number % 4 == 0, named(crowded, number // 4), named(common, number - number // 4 - 1))
    mixed = jax.random.permutation(jax.random.fold_in(own, 3), count)
    source_of, sink = mixed[0:count // 2 * 2:2], mixed[1:count // 2 * 2:2]
    room = jnp.minimum(tallies[source_of] - 1, most - tallies[sink]) // 2
    room = jnp.where((source_of == order[0]) | (sink == order[0]) | (tallies[sink] == 0), 0, jnp.maximum(room, 0))
    moved = jax.random.randint(jax.random.fold_in(own, 4), (count // 2,), 0, 1 << 20) % (room + 1)
    tallies = tallies.at[source_of].add(-moved).at[sink].add(moved)
    items = jnp.searchsorted(jnp.cumsum(tallies), jnp.arange(rows * top), side="right").astype(jnp.int32)
    table = items.reshape(top, rows).T
    table = table[jax.random.permutation(jax.random.fold_in(own, 1), rows)]
    offset_by = jax.random.randint(jax.random.fold_in(own, 2), (rows, 1), 0, top)
    return jnp.take_along_axis(table, (jnp.arange(top)[None, :] + offset_by) % top, axis=1)


def load_shares(number_of, total, most, slope, full):
    portions = [(1 << 20) // math.isqrt(standing ** slope) + 1 for standing in range(1, number_of + 1)]
    largest = most if full else min(most, max(-(-total // number_of), total * portions[0] // sum(portions)))
    least = 1 if total - largest >= number_of - 1 else 0
    holding, rest = [largest] + [least] * (number_of - 1), total - largest - least * (number_of - 1)
    while rest > 0:
        free = [i for i in range(1, number_of) if holding[i] < largest] or [i for i in range(1, number_of) if holding[i] < most]
        mass, left = sum([portions[i] for i in free]), rest
        for i in free:
            more = min(most - holding[i], max(1, left * portions[i] // mass), rest)
            holding[i] = holding[i] + more
            rest = rest - more
    return np.array(holding)


def bell_draw(stream_key, shape, width, most, cuts=(), kind=jnp.bfloat16):
    factor_of = shard_levels(stream_key, shape, cuts, -0.22, 0.18) if cuts else 1.0
    drawn = jax.random.normal(stream_key, shape, jnp.float32) * width * factor_of
    return jnp.minimum(jnp.maximum(drawn, -most), most).astype(kind)


def setup_inputs(seed: int = 0) -> dict:
    splits = jax.random.split(jax.random.key(seed), 11)
    nbr_feats = bell_draw(splits[0], (NEIGHBOURS, F), 1.0, 6.0, ((0, 1024),), jnp.float32)
    tgt_feats = bell_draw(splits[1], (TARGETS, F), 1.0, 6.0, ((0, 1024),), jnp.float32)
    msg_weight = bell_draw(splits[2], (F, F), F ** -0.5, 0.25)
    comb_weight = bell_draw(splits[3], (2 * F, F), (2 * F) ** -0.5, 0.1875)
    head_gain = draw_head_gain(jax.random.fold_in(splits[10], 71), 0)
    owners_keys = jax.random.split(jax.random.fold_in(splits[5], 1), TARGETS // TGT_DEV)
    owners_turns = jax.random.permutation(jax.random.fold_in(splits[5], 3), TARGETS // TGT_DEV)
    owners = jax.vmap(lambda own, number: deal_out(jax.random.fold_in(splits[5], 2), own, number, TGT_DEV, N_NODE, NBR, CAP, 2))(owners_keys, owners_turns).reshape((TARGETS, NBR))
    serve_rows = touch_ends(jax.random.randint(splits[6], (DEVICES, N_NODE, CAP), 0, ROWS_DEV), jax.random.fold_in(splits[6], 1), 0, ROWS_DEV - 1).astype(jnp.int32)
    importance = touch_ends(jax.random.randint(splits[7], (TARGETS, NBR), 1, 33), jax.random.fold_in(splits[7], 1), 1, 32).astype(jnp.int32)
    labels = touch_ends(jax.random.randint(splits[8], (TARGETS,), 0, TASKS), jax.random.fold_in(splits[8], 1), 0, TASKS - 1).astype(jnp.int32)
    positives = touch_ends(jax.random.randint(splits[9], (TARGETS,), 0, GROUPT), jax.random.fold_in(splits[9], 1), 0, GROUPT - 1).astype(jnp.int32)
    return dict(nbr_feats=nbr_feats, tgt_feats=tgt_feats, msg_weight=msg_weight, comb_weight=comb_weight, head_gain=head_gain, owners=owners, serve_rows=serve_rows, importance=importance, labels=labels, positives=positives)


eps = 1e-05

def silu_slope(value):
    logistic = jax.nn.sigmoid(value)
    return logistic * (1.0 + value * (1.0 - logistic))

def reference(nbr_feats, tgt_feats, msg_weight, comb_weight, head_gain, owners, serve_rows, importance, labels, positives):
    nbr_bf = nbr_feats.astype(jnp.bfloat16)
    msg_pre = jnp.dot(nbr_bf, msg_weight, preferred_element_type=jnp.float32)
    messages = jax.nn.silu(msg_pre).astype(jnp.bfloat16)
    owner_lists = owners.reshape(DEVICES, TGT_DEV * NBR).astype(jnp.int32)
    owner_hits = (owner_lists[:, :, None] == jnp.arange(N_NODE, dtype=jnp.int32)[None, None, :]).astype(jnp.int32)
    earlier = (jnp.cumsum(owner_hits, axis=1) - owner_hits).astype(jnp.int32)
    slot_index = lax.optimization_barrier(jnp.sum(earlier * owner_hits, axis=2)).astype(jnp.int32)
    device_ids = jnp.arange(DEVICES, dtype=jnp.int32)[:, None]
    reader_node = (device_ids // N_GRP).astype(jnp.int32)
    reader_grp = (device_ids % N_GRP).astype(jnp.int32)
    owner_device = (owner_lists * N_GRP + reader_grp).astype(jnp.int32)
    local_rows = serve_rows[owner_device, reader_node, slot_index].astype(jnp.int32)
    global_rows = (owner_device * ROWS_DEV + local_rows).reshape(TARGETS * NBR).astype(jnp.int32)
    weight_f = importance.astype(jnp.float32)
    weight_total = lax.optimization_barrier(jnp.sum(weight_f, axis=1))
    gathered = jnp.take(messages, global_rows, axis=0).reshape(TARGETS, NBR, F).astype(jnp.float32)
    aggregate = lax.optimization_barrier(jnp.sum(weight_f[:, :, None] * gathered, axis=1)) / weight_total[:, None]
    comb_in = jnp.concatenate([tgt_feats.astype(jnp.bfloat16), aggregate.astype(jnp.bfloat16)], axis=1)
    comb_pre = jnp.dot(comb_in, comb_weight, preferred_element_type=jnp.float32)
    hidden = jax.nn.silu(comb_pre)
    inv_norm = lax.rsqrt(lax.optimization_barrier(jnp.mean(hidden * hidden, axis=1)) + eps)
    embed = (hidden * inv_norm[:, None]).astype(jnp.bfloat16)
    embed_f = embed.astype(jnp.float32)
    gain_rows = jnp.take(head_gain, labels.astype(jnp.int32), axis=0)
    query = (embed_f * gain_rows).astype(jnp.bfloat16)
    query_g = query.astype(jnp.float32).reshape(N_NODE, GROUPT, F)
    embed_g = embed_f.reshape(N_NODE, GROUPT, F)
    scores = jnp.einsum('ntf,nsf->nts', query_g, embed_g) / F
    top_value = lax.optimization_barrier(jnp.max(scores, axis=2, keepdims=True))
    exp_terms = jnp.exp(scores - top_value)
    totals = lax.optimization_barrier(jnp.sum(exp_terms, axis=2, keepdims=True))
    pos_g = positives.reshape(N_NODE, GROUPT).astype(jnp.int32)
    picked = jnp.take_along_axis(scores, pos_g[:, :, None], axis=2)[:, :, 0]
    loss = (top_value[:, :, 0] + jnp.log(totals[:, :, 0]) - picked).reshape(TARGETS)
    column_ids = lax.broadcasted_iota(jnp.int32, scores.shape, 2)
    hit_mask = (column_ids == pos_g[:, :, None]).astype(jnp.float32)
    score_grad = ((exp_terms / totals - hit_mask) / GROUPT / F).astype(jnp.bfloat16)
    grad_f = score_grad.astype(jnp.float32)
    query_grad = jnp.einsum('nts,nsf->ntf', grad_f, embed_g).reshape(TARGETS, F)
    column_grad = jnp.einsum('nts,ntf->nsf', grad_f, query_g).reshape(TARGETS, F)
    embed_grad = query_grad * gain_rows + column_grad
    grad_head = jax.ops.segment_sum(query_grad * embed_f, labels.astype(jnp.int32), TASKS)
    inner = lax.optimization_barrier(jnp.sum(hidden * embed_grad, axis=1))
    cube = inv_norm * inv_norm * inv_norm
    hidden_grad = inv_norm[:, None] * embed_grad - hidden * (cube * inner / F)[:, None]
    pre_grad = (silu_slope(comb_pre) * hidden_grad).astype(jnp.bfloat16)
    grad_comb = jnp.dot(comb_in.T, pre_grad, preferred_element_type=jnp.float32)
    agg_grad = jnp.dot(pre_grad, comb_weight[F:].T, preferred_element_type=jnp.float32)
    share = weight_f / weight_total[:, None]
    msg_grad = (share[:, :, None] * agg_grad[:, None, :]).astype(jnp.bfloat16)
    row_grad = jnp.zeros((NEIGHBOURS, F), jnp.float32).at[global_rows].add(msg_grad.reshape(TARGETS * NBR, F).astype(jnp.float32))
    msg_pre_grad = (silu_slope(msg_pre) * row_grad).astype(jnp.bfloat16)
    grad_msg = jnp.dot(nbr_bf.T, msg_pre_grad, preferred_element_type=jnp.float32)
    return (loss, grad_msg, grad_comb, grad_head)
```

```python
import functools

import jax
import jax.numpy as jnp
from jax import lax
from jax.experimental import pallas as pl
from jax.experimental.pallas import tpu as pltpu
from jax.sharding import PartitionSpec as P

MESH = pl.DeviceIdType.MESH
F32, BF16, I32 = jnp.float32, jnp.bfloat16, jnp.int32
eps = 1e-05
LANES = 128
SPAN = 16
ROW = 8
FRONT = 16


def dot(left, right):
    return jnp.dot(left, right, preferred_element_type=F32)


def dot_nt(left, right):
    return lax.dot_general(left, right, (((1,), (1,)), ((), ())), preferred_element_type=F32)


def dot_tn(left, right):
    return lax.dot_general(left, right, (((0,), (0,)), ((), ())), preferred_element_type=F32)


def iota(shape, dim):
    return lax.broadcasted_iota(I32, shape, dim)


def ones_where(mask):
    return jnp.where(mask, 1.0, 0.0).astype(BF16)


def sigmoid(value):
    return 1.0 / (1.0 + jnp.exp(-value))


def silu_slope(value):
    logistic = sigmoid(value)
    return logistic * (1.0 + value * (1.0 - logistic))


def halves_stacked(value):
    mid = value.shape[1] // 2
    return jnp.concatenate([value[:, :mid], value[:, mid:]], axis=0)


def rows(start, size):
    return pl.ds(pl.multiple_of(start, size), size)


def as_column(row):
    return jnp.transpose(jnp.broadcast_to(row, (LANES, LANES)))


def greet(nodes, grps):
    node, grp = lax.axis_index("node"), lax.axis_index("grp")
    barrier = pltpu.get_barrier_semaphore()

    def hello_node(step, _):
        peer = (lax.rem(node + step, nodes), grp)
        pl.semaphore_signal(barrier, inc=1, device_id=peer, device_id_type=MESH)
        return 0

    def hello_grp(step, _):
        peer = (node, lax.rem(grp + step, grps))
        pl.semaphore_signal(barrier, inc=1, device_id=peer, device_id_type=MESH)
        return 0

    lax.fori_loop(1, nodes, hello_node, 0)
    lax.fori_loop(1, grps, hello_grp, 0)
    return lambda: pl.semaphore_wait(barrier, nodes + grps - 2)


class Exchange:
    def __init__(self, nodes, out_ref, in_ref, send_sem, recv_sem):
        self.nodes, self.planes = nodes, nodes // ROW
        self.out_ref, self.in_ref, self.send_sem, self.recv_sem = out_ref, in_ref, send_sem, recv_sem

    def peer(self, index, sign):
        me = lax.axis_index("node")
        dz = index % self.planes
        dy = (dz + index // self.planes) % ROW
        z = (me // ROW + self.planes + sign * dz) % self.planes
        return z * ROW + (me % ROW + ROW + sign * dy) % ROW

    def copy(self, index):
        at = rows(index * SPAN, SPAN)
        return pltpu.make_async_remote_copy(
            src_ref=self.out_ref.at[at, :],
            dst_ref=self.in_ref.at[at, :],
            send_sem=self.send_sem.at[index],
            recv_sem=self.recv_sem.at[index],
            device_id=(self.peer(index, 1), lax.axis_index("grp")),
            device_id_type=MESH,
        )

    def keep(self):
        self.in_ref[:SPAN, :] = self.out_ref[:SPAN, :]

    def start(self, first, last):
        lax.fori_loop(first, last, lambda i, _: (self.copy(i).start(), 0)[1], 0)

    def arrive(self, first, last):
        lax.fori_loop(first, last, lambda i, _: (self.copy(i).wait_recv(), 0)[1], 0)

    def finish(self):
        lax.fori_loop(1, self.nodes, lambda i, _: (self.copy(i).wait_send(), 0)[1], 0)


class Stage:
    def __init__(self, count, me, peer, source, landing, size, send_sem, recv_sem):
        self.count, self.me, self.peer, self.source = count, me, peer, source
        self.landing, self.size, self.send_sem, self.recv_sem = landing, size, send_sem, recv_sem

    def copy(self, to, place):
        return pltpu.make_async_remote_copy(
            src_ref=self.source(to),
            dst_ref=self.landing.at[rows(place * self.size, self.size), :],
            send_sem=self.send_sem.at[to],
            recv_sem=self.recv_sem.at[place],
            device_id=self.peer(to),
            device_id_type=MESH,
        )

    def each(self, act):
        def step(i, _):
            act(lax.rem(self.me + i, self.count))
            return 0

        lax.fori_loop(1, self.count, step, 0)

    def start(self):
        self.each(lambda to: self.copy(to, self.me).start())

    def arrive(self):
        self.each(lambda source: self.copy(source, source).wait_recv())

    def finish(self):
        self.each(lambda to: self.copy(to, self.me).wait_send())

    def total(self, own):
        def add(i, acc):
            source = lax.rem(self.me + i, self.count)
            return acc + self.landing[rows(source * self.size, self.size), :].astype(F32)

        return lax.fori_loop(1, self.count, add, own)


def to_pieces(value, ref):
    per = ref.shape[1] // LANES
    wide = value.shape[1] // LANES
    for k in range(value.shape[0] // 8 * wide):
        r, c = divmod(k, wide)
        piece, place = divmod(k, per)
        ref[piece * 8 : piece * 8 + 8, place * LANES : place * LANES + LANES] = value[
            r * 8 : r * 8 + 8, c * LANES : c * LANES + LANES
        ]


def from_pieces(ref, shape):
    per = ref.shape[1] // LANES
    wide = shape[1] // LANES
    bands = []
    for r in range(shape[0] // 8):
        band = []
        for c in range(wide):
            piece, place = divmod(r * wide + c, per)
            band.append(ref[piece * 8 : piece * 8 + 8, place * LANES : place * LANES + LANES])
        bands.append(jnp.concatenate(band, axis=1))
    return jnp.concatenate(bands, axis=0)


class NodeSum:
    def __init__(self, nodes, pieces, z_in, mine, y_in, full, sems):
        node, grp = lax.axis_index("node"), lax.axis_index("grp")
        planes = nodes // ROW
        self.z, self.y = node // ROW, lax.rem(node, ROW)
        z, y = self.z, self.y
        self.pieces, self.mine, self.y_in, self.full = pieces, mine, y_in, full

        def z_peer(to):
            return (to * ROW + y, grp)

        def y_peer(to):
            return (z * ROW + to, grp)

        self.first = Stage(planes, z, z_peer, lambda to: pieces.at[rows(to * 8, 8), :], z_in, 8, sems[0], sems[1])
        self.second = Stage(ROW, y, y_peer, lambda to: mine, y_in, 8, sems[2], sems[3])
        self.third = Stage(planes, z, z_peer, lambda to: full.at[rows(z * 8, 8), :], full, 8, sems[4], sems[5])

    def begin(self, value):
        if self.pieces.shape[0] * self.pieces.shape[1] > value.shape[0] * value.shape[1]:
            self.pieces[...] = jnp.zeros_like(self.pieces)
        to_pieces(value, self.pieces)
        self.first.start()

    def over_y(self):
        self.first.arrive()
        own = self.first.total(self.pieces[rows(self.z * 8, 8), :])
        self.mine[...] = own
        self.y_in[rows(self.y * 8, 8), :] = own
        self.second.start()

    def gather(self):
        self.second.arrive()
        total = self.y_in[:8, :]
        for k in range(1, ROW):
            total = total + self.y_in[k * 8 : k * 8 + 8, :]
        self.full[rows(self.z * 8, 8), :] = total
        self.third.start()

    def end(self):
        self.third.arrive()

    def finish(self):
        for stage in (self.first, self.second, self.third):
            stage.finish()


class Ring:
    def __init__(self, grps, all_ref, size, send_sem, recv_sem):
        node, me = lax.axis_index("node"), lax.axis_index("grp")
        self.node, self.me, self.all_ref, self.size = node, me, all_ref, size
        self.send_sem, self.recv_sem = send_sem, recv_sem
        self.chips, self.core, self.chip = grps // 2, lax.rem(me, 2), me // 2
        self.hops = self.chips // 2
        self.index, self.started = {}, []
        for side in (0, 1):
            for hop in range(1, self.hops + 1):
                for piece in (0, 1):
                    if hop < self.hops or piece == side:
                        self.index["link", side, hop, piece] = len(self.index)
        for key in list(self.index):
            self.index[("core",) + key[1:]] = len(self.index)
        for piece in (0, 1):
            self.index["core", 0, 0, piece] = len(self.index)

    def at_chip(self, steps):
        return lax.rem(self.chip + self.chips + steps, self.chips) * 2 + self.core

    def origin(self, side, hop):
        return self.at_chip(-hop if side == 0 else hop)

    def copy(self, key):
        kind, side, hop, piece = key
        origin = self.origin(side, hop - 1 if kind == "link" else hop)
        half = self.size // 2
        at = rows(origin * self.size + piece * half, half)
        to = self.at_chip(1 if side == 0 else -1) if kind == "link" else self.chip * 2 + 1 - self.core
        return pltpu.make_async_remote_copy(
            src_ref=self.all_ref.at[at, :],
            dst_ref=self.all_ref.at[at, :],
            send_sem=self.send_sem.at[self.index[key]],
            recv_sem=self.recv_sem.at[self.index[key]],
            device_id=(self.node, to),
            device_id_type=MESH,
        )

    def start(self, *key):
        if key in self.index:
            self.copy(key).start()
            self.started.append(key)

    def arrive(self, *key):
        if key in self.index:
            self.copy(key).wait_recv()

    def begin(self):
        for piece in (0, 1):
            for side in (0, 1):
                self.start("link", side, 1, piece ^ side)
        for piece in (0, 1):
            self.start("core", 0, 0, piece)

    def step(self, hop):
        for piece in (0, 1):
            for side in (0, 1):
                key = (side, hop, piece ^ side)
                self.arrive("link", *key)
                self.start("link", side, hop + 1, piece ^ side)
                if ("link", *key) in self.index:
                    self.start("core", *key)

    def other(self, hop):
        for side in (0, 1):
            for piece in (0, 1):
                if hop or side == 0:
                    self.arrive("core", side, hop, piece)

    def finish(self):
        for key in self.started:
            self.copy(key).wait_send()


def tower_kernel(
    nodes, grps, nbr_ref, tgt_ref, msgw_ref, combw_ref, gain_ref, served_ref, owners_ref, weight_ref, labels_ref, pos_ref,
    loss_ref, gmsg_ref, gcomb_ref, ghead_ref,
    msg_ref, msg2_ref, bf_ref, slope_ref, serve_ref,
    out_ref, in_ref, send_sem, recv_sem, a1_ref, a2_ref, at1_ref, at2_ref, front_ref, back_ref, comb_in_ref, pre_ref,
    all_ref, query_ref, gains_ref, rt_ref, ct_ref, ring_send, ring_recv, stat_ref, stat_send, stat_recv,
    out2_ref, in2_ref, send2_sem, recv2_sem, acc_ref, acc2_ref,
    cpart_ref, cland_ref, cpart_send, cpart_recv, cpieces, cz_in, cmine, cy_in, cfull, c0, c1, c2, c3, c4, c5,
    mpart_ref, pair_ref, pair_send, pair_recv, mhalf_ref, mland_ref, mx_send, mx_recv,
    mpieces, mz_in, mmine, my_in, mfull, m0, m1, m2, m3, m4, m5,
):
    ready = greet(nodes, grps)
    node, me = lax.axis_index("node"), lax.axis_index("grp")
    feat, tgts, pins = msgw_ref.shape[0], tgt_ref.shape[0], nbr_ref.shape[0]
    half, planes, span, group = feat // 2, nodes // ROW, nodes * SPAN, tgts * grps
    chunks = span // LANES
    per = LANES // SPAN
    lane = iota((LANES, LANES), 1)
    sub = iota((LANES, LANES), 0)

    def message(tile, _):
        at = rows(tile * LANES, LANES)
        nbr = nbr_ref[at, :].astype(BF16)
        bf_ref[at, :] = nbr
        pre = dot(nbr, msgw_ref[...])
        slope_ref[at, :] = pre
        msg = (pre * sigmoid(pre)).astype(BF16)
        msg_ref[at, :] = msg
        msg2_ref[at, :] = msg[:, :half]
        msg2_ref[rows(pins + tile * LANES, LANES), :] = msg[:, half:]
        return 0

    lax.fori_loop(0, pins // LANES, message, 0)
    serve_ref[...] = jnp.zeros_like(serve_ref)
    serve_ref[: served_ref.shape[0], : served_ref.shape[1]] = served_ref[...]
    forth = Exchange(nodes, out_ref, in_ref, send_sem, recv_sem)
    back = Exchange(nodes, out2_ref, in2_ref, send2_sem, recv2_sem)

    def keys_of(chunk, sign):
        peers = forth.peer(sub // SPAN + chunk * per, sign)
        pick = ones_where(lane == peers)
        table = serve_ref[...]
        upper = (table // 2).astype(F32).astype(BF16)
        lower = (table % 2).astype(F32).astype(BF16)
        listed = dot(pick, upper) * 2.0 + dot(pick, lower)
        place = sub % SPAN
        key1 = jnp.sum(jnp.where(lane == place, listed, 0.0), axis=1, keepdims=True)
        key2 = jnp.sum(jnp.where(lane == FRONT + place % 8, listed, 0.0), axis=1, keepdims=True)
        key1 = jnp.broadcast_to(key1, (LANES, LANES))
        key2 = jnp.broadcast_to(key2, (LANES, LANES)) + jnp.where(place >= 8, float(pins), 0.0)
        return key1.astype(I32), key2.astype(I32)

    ready()

    def serve(chunk, _):
        at = rows(chunk * LANES, LANES)
        key1, key2 = keys_of(chunk, 1)
        pick1 = jnp.concatenate([ones_where(key1 == lane + c * LANES) for c in range(pins // LANES)], 1)
        pick2 = jnp.concatenate([ones_where(key2 == lane + c * LANES) for c in range(2 * pins // LANES)], 1)
        out_ref[at, :feat] = dot(pick1, msg_ref[...]).astype(BF16)
        out_ref[at, feat:] = dot(pick2, msg2_ref[...]).astype(BF16)
        forth.start(jnp.maximum(chunk * per, 1), chunk * per + per)
        return 0

    lax.fori_loop(0, chunks, serve, 0)
    forth.keep()

    hits_t = jnp.zeros((LANES, tgts), F32)
    weights_t = jnp.zeros((LANES, tgts), F32)
    for k in range(owners_ref.shape[0]):
        hit = owners_ref[k : k + 1, :] == sub
        hits_t = hits_t + jnp.where(hit, 1.0, 0.0)
        weights_t = weights_t + jnp.where(hit, weight_ref[k : k + 1, :].astype(F32), 0.0)
    above = ones_where(sub < lane)
    earlier_t = dot(hits_t.astype(BF16), above)
    weights = jnp.transpose(weights_t)
    total = jnp.sum(weights, axis=1, keepdims=True)
    earlier = jnp.transpose(earlier_t).astype(BF16)
    weights, earlier_t, weights_t = weights.astype(BF16), earlier_t.astype(BF16), weights_t.astype(BF16)

    def weigh(chunk, _):
        at = rows(chunk * LANES, LANES)
        spread = ones_where(sub == forth.peer(lane // SPAN + chunk * per, -1))
        slot, weight = dot(earlier, spread), dot(weights, spread)
        place = lane % SPAN
        a1_ref[:, at] = jnp.where(slot == place.astype(F32), weight, 0.0).astype(BF16)
        late = jnp.where(slot == (FRONT + place % 8).astype(F32), weight, 0.0)
        a2_ref[:tgts, at] = jnp.where(place < 8, late, 0.0).astype(BF16)
        a2_ref[tgts:, at] = jnp.where(place >= 8, late, 0.0).astype(BF16)
        spread = ones_where(lane == forth.peer(sub // SPAN + chunk * per, 1))
        slot, weight = dot(spread, earlier_t), dot(spread, weights_t)
        place = sub % SPAN
        at1_ref[at, :] = jnp.where(slot == place.astype(F32), weight, 0.0).astype(BF16)
        late = jnp.where(slot == (FRONT + place % 8).astype(F32), weight, 0.0)
        at2_ref[at, :tgts] = jnp.where(place < 8, late, 0.0).astype(BF16)
        at2_ref[at, tgts:] = jnp.where(place >= 8, late, 0.0).astype(BF16)
        return 0

    lax.fori_loop(0, chunks, weigh, 0)

    tgt_bf = tgt_ref[...].astype(BF16)
    comb_in_ref[:, :feat] = tgt_bf
    pre_ref[...] = dot(tgt_bf, combw_ref[:feat, :])

    def slopes(tile, _):
        at = rows(tile * LANES, LANES)
        slope_ref[at, :] = silu_slope(slope_ref[at, :])
        return 0

    lax.fori_loop(0, pins // LANES, slopes, 0)
    gain = gain_ref[...]
    gain_hi = gain.astype(BF16).astype(F32)
    gain_mid = (gain - gain_hi).astype(BF16).astype(F32)
    gain_lo = gain - gain_hi - gain_mid
    tasks = gain.shape[0]
    gain3 = jnp.concatenate(
        [gain_hi, gain_mid, gain_lo, jnp.zeros((LANES - 3 * tasks, feat), F32)], axis=0
    ).astype(BF16)

    def gains(block, _):
        label = as_column(labels_ref[pl.ds(block, 1), :])
        pick = ones_where((label == lane % tasks) & (lane < 3 * tasks))
        gains_ref[rows(block * tgts, tgts), :] = dot(pick, gain3)
        return 0

    lax.fori_loop(0, grps, gains, 0)
    front_ref[...] = jnp.zeros_like(front_ref)
    back_ref[...] = jnp.zeros_like(back_ref)
    acc_ref[...] = jnp.zeros_like(acc_ref)
    acc2_ref[...] = jnp.zeros_like(acc2_ref)

    def collect(chunk, _):
        at = rows(chunk * LANES, LANES)
        forth.arrive(jnp.maximum(chunk * per, 1), chunk * per + per)
        front_ref[...] += dot(a1_ref[:, at], in_ref[at, :feat])
        back_ref[...] += dot(a2_ref[:, at], in_ref[at, feat:])
        return 0

    lax.fori_loop(0, chunks, collect, 0)
    aggregate = front_ref[...] + jnp.concatenate([back_ref[:tgts, :], back_ref[tgts:, :]], axis=1)
    agg_bf = (aggregate / total).astype(BF16)
    comb_in_ref[:, feat:] = agg_bf
    comb_pre = pre_ref[...] + dot(agg_bf, combw_ref[feat:, :])
    pre_ref[...] = comb_pre
    hidden = comb_pre * sigmoid(comb_pre)
    inv_norm = lax.rsqrt(jnp.mean(hidden * hidden, axis=1, keepdims=True) + eps)
    embed = (hidden * inv_norm).astype(BF16)

    own = rows(me * tgts, tgts)
    all_ref[own, :] = embed
    ring = Ring(grps, all_ref, tgts, ring_send, ring_recv)
    ring.begin()
    own_gain = gains_ref[own, :]
    own_query = (embed.astype(F32) * own_gain).astype(BF16)

    def score(block):
        at = rows(block * tgts, tgts)
        block_embed = all_ref[at, :]
        block_query = (block_embed.astype(F32) * gains_ref[at, :]).astype(BF16)
        query_ref[at, :] = block_query
        rt_ref[at, :] = dot_nt(block_embed, own_query) / feat
        ct_ref[at, :] = dot_nt(all_ref[own, :], block_query) / feat

    score(me)
    for hop in range(1, ring.hops + 1):
        ring.step(hop)
        ring.other(hop - 1)
        if hop < ring.hops:
            score(ring.origin(0, hop))
            score(ring.origin(1, hop))
        else:
            score(ring.origin(0, hop))
        for side in (0, 1) if hop > 1 else (0,):
            score(ring.origin(side, hop - 1) + 1 - 2 * ring.core)
    ring.other(ring.hops)
    score(ring.origin(0, ring.hops) + 1 - 2 * ring.core)

    scores = rt_ref[...]
    top = jnp.max(scores, axis=0, keepdims=True)
    terms = jnp.exp(scores - top)
    norm = jnp.sum(terms, axis=0, keepdims=True)
    own_stat = rows(me * 8, 8)
    stat_ref[own_stat, :] = jnp.concatenate(
        [jnp.broadcast_to(top, (4, LANES)), jnp.broadcast_to(norm, (4, LANES))], axis=0
    )
    stats = Stage(grps, me, lambda to: (node, to), lambda to: stat_ref.at[own_stat, :], stat_ref, 8, stat_send, stat_recv)
    stats.start()
    hit = jnp.where(iota((group, tgts), 0) == pos_ref[pl.ds(me, 1), :], 1.0, 0.0)
    picked = jnp.sum(scores * hit, axis=0, keepdims=True)
    loss_ref[...] = top + jnp.log(norm) - picked
    grad = ((terms / norm - hit) / group / feat).astype(BF16)
    query_grad = dot_tn(grad, all_ref[...])
    stats.arrive()

    def column(block, acc):
        at = rows(block * tgts, tgts)
        stat = stat_ref[rows(block * 8, 8), :]
        terms = jnp.exp(ct_ref[at, :] - stat[0:1, :]) / stat[4:5, :]
        mine = iota((tgts, LANES), 0) + me * tgts == pos_ref[pl.ds(block, 1), :]
        grad = ((terms - jnp.where(mine, 1.0, 0.0)) / group / feat).astype(BF16)
        return acc + dot(grad, query_ref[at, :])

    column_grad = lax.fori_loop(0, grps, column, jnp.zeros((tgts, feat), F32))
    embed_grad = query_grad * own_gain + column_grad
    logistic = sigmoid(comb_pre)
    inner = jnp.sum(hidden * embed_grad, axis=1, keepdims=True)
    cube = inv_norm * inv_norm * inv_norm
    hidden_grad = inv_norm * embed_grad - hidden * (cube * inner / feat)
    slope = logistic * (1.0 + comb_pre * (1.0 - logistic))
    pre_grad = (slope * hidden_grad).astype(BF16)
    agg = dot_nt(pre_grad, combw_ref[feat:, :]) / total

    agg_hi = agg.astype(BF16)
    agg_lo = (agg - agg_hi.astype(F32)).astype(BF16)
    both = jnp.concatenate([agg_hi, agg_lo], axis=0)
    both2 = jnp.concatenate([halves_stacked(agg_hi), halves_stacked(agg_lo)], axis=0)

    def give(chunk, _):
        at = rows(chunk * LANES, LANES)
        w1, w2 = at1_ref[at, :], at2_ref[at, :]
        out2_ref[at, :feat] = dot(jnp.concatenate([w1, w1], axis=1), both).astype(BF16)
        out2_ref[at, feat:] = dot(jnp.concatenate([w2, w2], axis=1), both2).astype(BF16)
        back.start(jnp.maximum(chunk * per, 1), chunk * per + per)
        return 0

    lax.fori_loop(0, chunks, give, 0)
    back.keep()

    cols = feat // grps
    cpart_ref[:, : 2 * feat] = dot_tn(pre_grad, comb_in_ref[...]).astype(BF16)
    pick = ones_where(as_column(labels_ref[pl.ds(me, 1), :]) == lane)
    head = query_grad * embed.astype(F32)
    head_hi = head.astype(BF16)
    head_lo = (head - head_hi.astype(F32)).astype(BF16)
    cpart_ref[:, 2 * feat :] = (dot_tn(head_hi, pick) + dot_tn(head_lo, pick)).astype(BF16)
    comb_sum = Stage(
        grps, me, lambda to: (node, to), lambda to: cpart_ref.at[rows(to * cols, cols), :], cland_ref, cols, cpart_send, cpart_recv
    )
    comb_sum.start()
    comb_full = NodeSum(nodes, cpieces, cz_in, cmine, cy_in, cfull, (c0, c1, c2, c3, c4, c5))
    msg_full = NodeSum(nodes, mpieces, mz_in, mmine, my_in, mfull, (m0, m1, m2, m3, m4, m5))

    def take(chunk, _):
        at = rows(chunk * LANES, LANES)
        key1, key2 = keys_of(chunk, -1)
        key1, key2 = jnp.transpose(key1), jnp.transpose(key2)
        spread1 = jnp.concatenate([ones_where(key1 == sub + c * LANES) for c in range(pins // LANES)], 0)
        spread2 = jnp.concatenate([ones_where(key2 == sub + c * LANES) for c in range(2 * pins // LANES)], 0)
        back.arrive(jnp.maximum(chunk * per, 1), chunk * per + per)
        acc_ref[...] += dot(spread1, in2_ref[at, :feat])
        acc2_ref[...] += dot(spread2, in2_ref[at, feat:])
        return 0

    lax.fori_loop(0, chunks - 2, take, 0)
    comb_sum.arrive()
    comb_full.begin(comb_sum.total(cpart_ref[rows(me * cols, cols), :].astype(F32)))
    lax.fori_loop(chunks - 2, chunks, take, 0)

    row_grad = acc_ref[...] + jnp.concatenate([acc2_ref[:pins, :], acc2_ref[pins:, :]], axis=1)
    msg_grad = (slope_ref[...] * row_grad).astype(BF16)
    part = dot_tn(msg_grad, bf_ref[...]).astype(BF16)
    for g in range(grps):
        first = (g % 2) * half + (g // 2) * cols
        mpart_ref[first : first + cols, :] = part[g * cols : g * cols + cols, :]
    core, chip = lax.rem(me, 2), me // 2
    pair = pltpu.make_async_remote_copy(
        src_ref=mpart_ref.at[rows((1 - core) * half, half), :],
        dst_ref=pair_ref,
        send_sem=pair_send,
        recv_sem=pair_recv,
        device_id=(node, chip * 2 + 1 - core),
        device_id_type=MESH,
    )
    pair.start()
    comb_full.over_y()
    pair.wait_recv()
    mhalf_ref[...] = (mpart_ref[rows(core * half, half), :].astype(F32) + pair_ref[...].astype(F32)).astype(BF16)
    over_x = Stage(
        grps // 2, chip, lambda to: (node, to * 2 + core), lambda to: mhalf_ref.at[rows(to * cols, cols), :], mland_ref, cols, mx_send, mx_recv
    )
    over_x.start()
    comb_full.gather()
    over_x.arrive()
    msg_full.begin(over_x.total(mhalf_ref[rows(chip * cols, cols), :].astype(F32)))
    comb_full.end()
    comb_value = from_pieces(cfull, (cols, 2 * feat + LANES))
    gcomb_ref[...] = comb_value[:, : 2 * feat]
    head_value = comb_value[:, 2 * feat :]
    if cols < LANES:
        head_value = jnp.concatenate([head_value, jnp.zeros((LANES - cols, LANES), F32)], axis=0)
    ghead_ref[...] = jnp.transpose(head_value)[:tasks, :]
    msg_full.over_y()
    msg_full.gather()
    forth.finish()
    ring.finish()
    stats.finish()
    back.finish()
    comb_sum.finish()
    comb_full.finish()
    pair.wait_send()
    over_x.finish()
    msg_full.end()
    gmsg_ref[...] = from_pieces(mfull, (cols, feat))
    msg_full.finish()


def body(
    nodes, grps, nbr_feats, tgt_feats, msg_weight, comb_weight, head_gain, owners, serve_rows, importance,
    labels, positives,
):
    pins, feat = nbr_feats.shape
    tgts, tasks = tgt_feats.shape[0], head_gain.shape[0]
    group, span, half = tgts * grps, nodes * SPAN, feat // 2
    cols, planes, chips = feat // grps, nodes // ROW, grps // 2
    hops = chips // 2
    links = 2 * max(2 * hops - 1, 0)
    block = feat + half
    wide = 2 * feat + LANES

    def vm(kind, *shape):
        return pltpu.VMEM(shape, kind)

    def dma(*shape):
        return pltpu.SemaphoreType.DMA(shape)

    def sum_scratch(width):
        per = -(-(cols // 8 * (width // LANES)) // planes) * LANES
        piece = [vm(F32, planes * 8, per), vm(F32, planes * 8, per), vm(F32, 8, per), vm(F32, ROW * 8, per), vm(F32, planes * 8, per)]
        return piece + [dma(planes), dma(planes), dma(ROW), dma(ROW), dma(planes), dma(planes)]

    scratch = [
        vm(BF16, pins, feat), vm(BF16, 2 * pins, half), vm(BF16, pins, feat), vm(F32, pins, feat), vm(I32, LANES, LANES),
        vm(BF16, span, block), vm(BF16, span, block), dma(nodes), dma(nodes),
        vm(BF16, tgts, span), vm(BF16, 2 * tgts, span), vm(BF16, span, tgts), vm(BF16, span, 2 * tgts),
        vm(F32, tgts, feat), vm(F32, 2 * tgts, half), vm(BF16, tgts, 2 * feat), vm(F32, tgts, feat),
        vm(BF16, group, feat), vm(BF16, group, feat), vm(F32, group, feat), vm(F32, group, tgts), vm(F32, group, tgts),
        dma(2 * links + 2), dma(2 * links + 2), vm(F32, grps * 8, LANES), dma(grps), dma(grps),
        vm(BF16, span, block), vm(BF16, span, block), dma(nodes), dma(nodes), vm(F32, pins, feat), vm(F32, 2 * pins, half),
        vm(BF16, feat, wide), vm(BF16, feat, wide), dma(grps), dma(grps), *sum_scratch(wide),
        vm(BF16, feat, feat), vm(BF16, half, feat), pltpu.SemaphoreType.DMA, pltpu.SemaphoreType.DMA,
        vm(BF16, half, feat), vm(BF16, half, feat), dma(chips), dma(chips), *sum_scratch(feat),
    ]
    args = (
        nbr_feats, tgt_feats, msg_weight, comb_weight, head_gain, serve_rows[0], owners.T, importance.T,
        labels.reshape(grps, tgts), positives.reshape(grps, tgts),
    )
    whole = pl.BlockSpec(memory_space=pltpu.VMEM)
    outs = [(1, tgts), (cols, feat), (cols, 2 * feat), (tasks, max(cols, LANES))]
    loss, grad_msg, grad_comb, grad_head = pl.pallas_call(
        functools.partial(tower_kernel, nodes, grps),
        name="tower",
        out_shape=[jax.ShapeDtypeStruct(shape, F32) for shape in outs],
        in_specs=[whole] * len(args),
        out_specs=[whole] * len(outs),
        scratch_shapes=scratch,
        compiler_params=pltpu.CompilerParams(
            collective_id=0, has_side_effects=True, vmem_limit_bytes=60 * 2**20
        ),
    )(*args)
    return loss.reshape(tgts), grad_msg.T, grad_comb.T, grad_head[:, :cols]


def solution(mesh):
    placed = (
        P(("node", "grp"), None),
        P(("node", "grp"), None),
        P(),
        P(),
        P(),
        P(("node", "grp"), None),
        P(("node", "grp"), None, None),
        P(("node", "grp"), None),
        P("node"),
        P("node"),
    )
    return jax.shard_map(
        functools.partial(body, mesh.shape["node"], mesh.shape["grp"]),
        mesh=mesh,
        in_specs=placed,
        out_specs=(P(("node", "grp")), P(None, "grp"), P(None, "grp"), P(None, "grp")),
        check_vma=False,
    )
```

```python
import functools

import jax
import jax.numpy as jnp
from jax import lax
from jax.experimental import pallas as pl
from jax.experimental.pallas import tpu as pltpu
from jax.sharding import PartitionSpec as P

MESH = pl.DeviceIdType.MESH
F32, BF16, I32 = jnp.float32, jnp.bfloat16, jnp.int32
eps = 1e-05
LANES = 128
ROW = 8


def dot(left, right):
    return jnp.dot(left, right, preferred_element_type=F32)


def dot_nt(left, right):
    return lax.dot_general(left, right, (((1,), (1,)), ((), ())), preferred_element_type=F32)


def dot_tn(left, right):
    return lax.dot_general(left, right, (((0,), (0,)), ((), ())), preferred_element_type=F32)


def iota(shape, dim):
    return lax.broadcasted_iota(I32, shape, dim)


def ones_where(mask):
    return jnp.where(mask, 1.0, 0.0).astype(BF16)


def sigmoid(value):
    return 1.0 / (1.0 + jnp.exp(-value))


def silu_slope(value):
    logistic = sigmoid(value)
    return logistic * (1.0 + value * (1.0 - logistic))


def rows(start, size):
    return pl.ds(pl.multiple_of(start, size), size)


def as_column(row):
    return jnp.transpose(jnp.broadcast_to(row, (LANES, LANES)))


def greet(nodes, grps):
    node, grp = lax.axis_index("node"), lax.axis_index("grp")
    barrier = pltpu.get_barrier_semaphore()

    def hello_node(step, _):
        peer = (lax.rem(node + step, nodes), grp)
        pl.semaphore_signal(barrier, inc=1, device_id=peer, device_id_type=MESH)
        return 0

    def hello_grp(step, _):
        peer = (node, lax.rem(grp + step, grps))
        pl.semaphore_signal(barrier, inc=1, device_id=peer, device_id_type=MESH)
        return 0

    lax.fori_loop(1, nodes, hello_node, 0)
    lax.fori_loop(1, grps, hello_grp, 0)
    return lambda: pl.semaphore_wait(barrier, nodes + grps - 2)


def offset(step, count):
    return lax.rem(jnp.where(lax.rem(step, 2) == 1, (step + 1) // 2, count - step // 2), count)


class Stage:
    def __init__(self, count, me, peer, source, landing, size, send_sem, recv_sem):
        self.count, self.me, self.peer, self.source = count, me, peer, source
        self.landing, self.size, self.send_sem, self.recv_sem = landing, size, send_sem, recv_sem

    def copy(self, to, place):
        return pltpu.make_async_remote_copy(
            src_ref=self.source(to),
            dst_ref=self.landing.at[rows(place * self.size, self.size), :],
            send_sem=self.send_sem.at[to],
            recv_sem=self.recv_sem.at[place],
            device_id=self.peer(to),
            device_id_type=MESH,
        )

    def each(self, act):
        def step(i, _):
            act(lax.rem(self.me + offset(i, self.count), self.count))
            return 0

        lax.fori_loop(1, self.count, step, 0)

    def start(self):
        self.each(lambda to: self.copy(to, self.me).start())

    def arrive(self):
        self.each(lambda source: self.copy(source, source).wait_recv())

    def finish(self):
        self.each(lambda to: self.copy(to, self.me).wait_send())

    def total(self, own):
        def add(i, acc):
            source = lax.rem(self.me + i, self.count)
            return acc + self.landing[rows(source * self.size, self.size), :].astype(F32)

        return lax.fori_loop(1, self.count, add, own)


def to_pieces(value, ref):
    per = ref.shape[1] // LANES
    wide = value.shape[1] // LANES
    for k in range(value.shape[0] // 8 * wide):
        r, c = divmod(k, wide)
        piece, place = divmod(k, per)
        ref[piece * 8 : piece * 8 + 8, place * LANES : place * LANES + LANES] = value[
            r * 8 : r * 8 + 8, c * LANES : c * LANES + LANES
        ]


def from_pieces(ref, shape):
    per = ref.shape[1] // LANES
    wide = shape[1] // LANES
    bands = []
    for r in range(shape[0] // 8):
        band = []
        for c in range(wide):
            piece, place = divmod(r * wide + c, per)
            band.append(ref[piece * 8 : piece * 8 + 8, place * LANES : place * LANES + LANES])
        bands.append(jnp.concatenate(band, axis=1))
    return jnp.concatenate(bands, axis=0)


class Path:
    def __init__(self, nodes, y_first, cap, refs, sems):
        node, self.grp = lax.axis_index("node"), lax.axis_index("grp")
        planes = nodes // ROW
        z, y = node // ROW, lax.rem(node, ROW)
        self.y_first = y_first
        self.firsts, self.seconds = (ROW, planes) if y_first else (planes, ROW)
        self.me1, self.me2 = (y, z) if y_first else (z, y)
        self.block = cap * self.seconds
        (self.tab, self.ws, self.es, self.wt, self.et, self.a, self.at, self.pt, self.out, self.inn, self.sums, self.sent, self.land,
         self.agg, self.out2, self.in2) = refs
        block, me1, me2 = self.block, self.me1, self.me2
        firsts, seconds, peer1, peer2 = self.firsts, self.seconds, self.peer1, self.peer2

        def own_tab(to):
            return self.tab.at[rows(me2 * 16, 16), :]

        def own_agg(to):
            return self.agg.at[rows(me2 * LANES, LANES), :]

        self.tables = Stage(seconds, me2, peer2, own_tab, self.tab, 16, sems[0], sems[1])
        self.rows_out = Stage(firsts, me1, peer1, lambda to: self.out.at[rows(to * block, block), :], self.inn, block, sems[2], sems[3])
        self.sums_out = Stage(seconds, me2, peer2, lambda to: self.sent.at[rows(to * LANES, LANES), :], self.land, LANES, sems[4], sems[5])
        self.agg_out = Stage(seconds, me2, peer2, own_agg, self.agg, LANES, sems[6], sems[7])
        self.rows_back = Stage(firsts, me1, peer1, lambda to: self.out2.at[rows(to * block, block), :], self.in2, block, sems[8], sems[9])

    def node_of(self, first, second):
        return second * ROW + first if self.y_first else first * ROW + second

    def peer1(self, to):
        return (self.node_of(to, self.me2), self.grp)

    def peer2(self, to):
        return (self.node_of(self.me1, to), self.grp)

    def first(self, step):
        return lax.rem(self.me1 + offset(step, self.firsts), self.firsts)

    def put_tables(self, owners, weights):
        self.tab[rows(self.me2 * 16, 8), :] = owners
        self.tab[rows(self.me2 * 16 + 8, 8), :] = weights

    def key_column(self, first, upper, lower):
        sub, lane = iota((self.block, LANES), 0), iota((self.block, LANES), 1)
        pick = ones_where(lane == self.node_of(first, sub % self.seconds))
        listed = dot_nt(pick, upper) * 2.0 + dot_nt(pick, lower)
        return jnp.sum(jnp.where(lane == sub // self.seconds, listed, 0.0), axis=1, keepdims=True)

    def key_row(self, first, upper, lower):
        sub, lane = iota((self.block, LANES), 0), iota((self.block, LANES), 1)
        pick = ones_where(lane == self.node_of(first, sub % self.seconds))
        listed = dot_nt(upper, pick) * 2.0 + dot_nt(lower, pick)
        sub, lane = iota((LANES, self.block), 0), iota((LANES, self.block), 1)
        return jnp.sum(jnp.where(sub == lane // self.seconds, listed, 0.0), axis=0, keepdims=True)

    def serve(self, first, upper, lower, messages):
        key = self.key_column(first, upper, lower)
        pick = ones_where(key == iota((self.block, messages.shape[0]), 1).astype(F32))
        self.out[rows(first * self.block, self.block), :] = dot(pick, messages[...]).astype(BF16)

    def keep(self, out, inn):
        own = rows(self.me1 * self.block, self.block)
        inn[own, :] = out[own, :]

    def read_tables(self, above):
        sub = iota((LANES, LANES), 0)

        def read(second, _):
            hits = jnp.zeros((LANES, LANES), F32)
            weights = jnp.zeros((LANES, LANES), F32)
            for k in range(8):
                hit = self.tab[pl.ds(second * 16 + k, 1), :] == sub
                hits = hits + jnp.where(hit, 1.0, 0.0)
                weights = weights + jnp.where(hit, self.tab[pl.ds(second * 16 + 8 + k, 1), :].astype(F32), 0.0)
            earlier = dot(hits.astype(BF16), above)
            at = rows(second * LANES, LANES)
            self.wt[:, at] = weights
            self.et[:, at] = earlier
            self.ws[at, :] = jnp.transpose(weights).astype(BF16)
            self.es[at, :] = jnp.transpose(earlier).astype(BF16)
            return 0

        lax.fori_loop(0, self.seconds, read, 0)

    def weigh(self, first):
        tall = self.seconds * LANES
        owner = self.node_of(first, self.me2)
        spread = ones_where(iota((LANES, self.block), 0) == owner)
        weight, slot = dot(self.ws[...], spread), dot(self.es[...], spread)
        sub, lane = iota((tall, self.block), 0), iota((tall, self.block), 1)
        mine = (lane % self.seconds == sub // LANES) & (slot == (lane // self.seconds).astype(F32))
        self.a[first] = jnp.where(mine, weight, 0.0).astype(BF16)

    def weigh_back(self, first):
        tall = self.seconds * LANES
        owner = self.node_of(first, self.me2)
        weight, slot = self.wt[pl.ds(owner, 1), :], self.et[pl.ds(owner, 1), :]
        sub, lane = iota((self.block, tall), 0), iota((self.block, tall), 1)
        mine = (sub % self.seconds == lane // LANES) & (slot == (sub // self.seconds).astype(F32))
        self.at[first] = jnp.where(mine, weight, 0.0).astype(BF16)

    def spread(self, first, upper, lower):
        key = self.key_row(first, upper, lower)
        self.pt[first] = ones_where(iota((self.pt.shape[1], self.block), 0).astype(F32) == key)

    def finish(self):
        for stage in (self.tables, self.rows_out, self.sums_out, self.agg_out, self.rows_back):
            stage.finish()


class NodeSum:
    def __init__(self, nodes, pieces, z_in, mine, y_in, full, sems):
        node, grp = lax.axis_index("node"), lax.axis_index("grp")
        planes = nodes // ROW
        self.z, self.y = node // ROW, lax.rem(node, ROW)
        z, y = self.z, self.y
        self.pieces, self.mine, self.y_in, self.full = pieces, mine, y_in, full

        def z_peer(to):
            return (to * ROW + y, grp)

        def y_peer(to):
            return (z * ROW + to, grp)

        self.first = Stage(planes, z, z_peer, lambda to: pieces.at[rows(to * 8, 8), :], z_in, 8, sems[0], sems[1])
        self.second = Stage(ROW, y, y_peer, lambda to: mine, y_in, 8, sems[2], sems[3])
        self.third = Stage(planes, z, z_peer, lambda to: full.at[rows(z * 8, 8), :], full, 8, sems[4], sems[5])

    def begin(self, value):
        if self.pieces.shape[0] * self.pieces.shape[1] > value.shape[0] * value.shape[1]:
            self.pieces[...] = jnp.zeros_like(self.pieces)
        to_pieces(value, self.pieces)
        self.first.start()

    def over_y(self):
        self.first.arrive()
        own = self.first.total(self.pieces[rows(self.z * 8, 8), :])
        self.mine[...] = own
        self.y_in[rows(self.y * 8, 8), :] = own
        self.second.start()

    def gather(self):
        self.second.arrive()
        total = self.y_in[:8, :]
        for k in range(1, ROW):
            total = total + self.y_in[k * 8 : k * 8 + 8, :]
        self.full[rows(self.z * 8, 8), :] = total
        self.third.start()

    def end(self):
        self.third.arrive()

    def finish(self):
        for stage in (self.first, self.second, self.third):
            stage.finish()


class Ring:
    def __init__(self, grps, all_ref, size, send_sem, recv_sem):
        node, me = lax.axis_index("node"), lax.axis_index("grp")
        self.node, self.me, self.all_ref, self.size = node, me, all_ref, size
        self.send_sem, self.recv_sem = send_sem, recv_sem
        self.chips, self.core, self.chip = grps // 2, lax.rem(me, 2), me // 2
        self.hops = self.chips // 2
        self.index, self.started = {}, []
        for side in (0, 1):
            for hop in range(1, self.hops + 1):
                for piece in (0, 1):
                    if hop < self.hops or piece == side:
                        self.index["link", side, hop, piece] = len(self.index)
        for key in list(self.index):
            self.index[("core",) + key[1:]] = len(self.index)
        for piece in (0, 1):
            self.index["core", 0, 0, piece] = len(self.index)

    def at_chip(self, steps):
        return lax.rem(self.chip + self.chips + steps, self.chips) * 2 + self.core

    def origin(self, side, hop):
        return self.at_chip(-hop if side == 0 else hop)

    def copy(self, key):
        kind, side, hop, piece = key
        origin = self.origin(side, hop - 1 if kind == "link" else hop)
        half = self.size // 2
        at = rows(origin * self.size + piece * half, half)
        to = self.at_chip(1 if side == 0 else -1) if kind == "link" else self.chip * 2 + 1 - self.core
        return pltpu.make_async_remote_copy(
            src_ref=self.all_ref.at[at, :],
            dst_ref=self.all_ref.at[at, :],
            send_sem=self.send_sem.at[self.index[key]],
            recv_sem=self.recv_sem.at[self.index[key]],
            device_id=(self.node, to),
            device_id_type=MESH,
        )

    def start(self, *key):
        if key in self.index:
            self.copy(key).start()
            self.started.append(key)

    def arrive(self, *key):
        if key in self.index:
            self.copy(key).wait_recv()

    def begin(self):
        for piece in (0, 1):
            for side in (0, 1):
                self.start("link", side, 1, piece ^ side)
        for piece in (0, 1):
            self.start("core", 0, 0, piece)

    def step(self, hop):
        for piece in (0, 1):
            for side in (0, 1):
                key = (side, hop, piece ^ side)
                self.arrive("link", *key)
                self.start("link", side, hop + 1, piece ^ side)
                if ("link", *key) in self.index:
                    self.start("core", *key)

    def other(self, hop):
        for side in (0, 1):
            for piece in (0, 1):
                if hop or side == 0:
                    self.arrive("core", side, hop, piece)

    def finish(self):
        for key in self.started:
            self.copy(key).wait_send()


def tower_kernel(
    nodes, grps, nbr_ref, tgt_ref, msgw_ref, combw_ref, gain_ref, served_ref, owners_ref, weight_ref, labels_ref, pos_ref,
    loss_ref, mfull, cfull,
    msg0_ref, msg1_ref, bf_ref, slope_ref, upper_ref, lower_ref, path0, path1, sems0, sems1,
    comb_in_ref, pre_ref,
    all_ref, query_ref, gains_ref, rt_ref, ct_ref, ring_send, ring_recv, stat_ref, stat_send, stat_recv,
    acc_ref,
    cpart_ref, cland_ref, cpart_send, cpart_recv, cpieces, cz_in, cmine, cy_in, c0, c1, c2, c3, c4, c5,
    mpart_ref, pair_ref, pair_send, pair_recv, mhalf_ref, mland_ref, mx_send, mx_recv,
    mpieces, mz_in, mmine, my_in, m0, m1, m2, m3, m4, m5,
):
    ready = greet(nodes, grps)
    node, me = lax.axis_index("node"), lax.axis_index("grp")
    feat, tgts, pins = msgw_ref.shape[0], tgt_ref.shape[0], nbr_ref.shape[0]
    half, group = feat // 2, tgts * grps
    lane = iota((LANES, LANES), 1)
    sub = iota((LANES, LANES), 0)
    cap = served_ref.shape[0]
    paths = [Path(nodes, True, cap, path0, sems0), Path(nodes, False, cap, path1, sems1)]
    longest = max(path.firsts for path in paths)
    halves = (msg0_ref, msg1_ref)

    def each_first(first, act):
        def turn(step, _):
            for which, path in enumerate(paths):
                if path.firsts == longest:
                    act(path, which, step)
                else:
                    pl.when(step < path.firsts)(functools.partial(act, path, which, step))
            return 0

        lax.fori_loop(first, longest, turn, 0)

    def message(tile, _):
        at = rows(tile * LANES, LANES)
        nbr = nbr_ref[at, :].astype(BF16)
        bf_ref[at, :] = nbr
        pre = dot(nbr, msgw_ref[...])
        slope_ref[at, :] = pre
        msg = (pre * sigmoid(pre)).astype(BF16)
        msg0_ref[at, :] = msg[:, :half]
        msg1_ref[at, :] = msg[:, half:]
        return 0

    lax.fori_loop(0, pins // LANES, message, 0)
    upper_ref[...] = jnp.zeros_like(upper_ref)
    lower_ref[...] = jnp.zeros_like(lower_ref)
    served = served_ref[...]
    upper_ref[:cap, : served.shape[1]] = (served // 2).astype(F32)
    lower_ref[:cap, : served.shape[1]] = (served % 2).astype(F32)
    upper, lower = upper_ref[...].astype(BF16), lower_ref[...].astype(BF16)
    for path in paths:
        path.put_tables(owners_ref[...], weight_ref[...])
    ready()
    for path in paths:
        path.tables.start()

    def serve(path, which, step):
        first = path.first(step)
        path.serve(first, upper, lower, halves[which])
        path.rows_out.copy(first, path.me1).start()

    each_first(1, serve)
    for path, messages in zip(paths, halves):
        path.serve(path.me1, upper, lower, messages)
        path.keep(path.out, path.inn)

    above = ones_where(sub < lane)
    for path in paths:
        path.tables.arrive()
        path.read_tables(above)
    each_first(0, lambda path, which, step: path.weigh(path.first(step)))
    for path in paths:
        path.sums[...] = dot(path.a[path.me1], path.inn[rows(path.me1 * path.block, path.block), :])
    own_path = paths[0]
    total = jnp.sum(own_path.ws[rows(own_path.me2 * LANES, LANES), :].astype(F32), axis=1, keepdims=True)
    tgt_bf = tgt_ref[...].astype(BF16)
    comb_in_ref[:, :feat] = tgt_bf
    pre_ref[...] = dot(tgt_bf, combw_ref[:feat, :])

    def collect(path, which, step):
        first = path.first(step)
        path.rows_out.copy(first, first).wait_recv()
        path.sums[...] += dot(path.a[first], path.inn[rows(first * path.block, path.block), :])

    each_first(1, collect)
    for path in paths:
        path.sent[...] = path.sums[...].astype(BF16)
        path.sums_out.start()

    each_first(0, lambda path, which, step: path.weigh_back(path.first(step)))
    gain = gain_ref[...]
    gain_hi = gain.astype(BF16).astype(F32)
    gain_mid = (gain - gain_hi).astype(BF16).astype(F32)
    gain_lo = gain - gain_hi - gain_mid
    tasks = gain.shape[0]
    gain3 = jnp.concatenate(
        [gain_hi, gain_mid, gain_lo, jnp.zeros((LANES - 3 * tasks, feat), F32)], axis=0
    ).astype(BF16)

    def gains(block, _):
        label = as_column(labels_ref[pl.ds(block, 1), :])
        pick = ones_where((label == lane % tasks) & (lane < 3 * tasks))
        gains_ref[rows(block * tgts, tgts), :] = dot(pick, gain3)
        return 0

    lax.fori_loop(0, grps, gains, 0)
    sums = []
    for path in paths:
        path.sums_out.arrive()
        sums.append(path.sums_out.total(path.sums[rows(path.me2 * LANES, LANES), :]))
    agg_bf = (jnp.concatenate(sums, axis=1) / total).astype(BF16)
    comb_in_ref[:, feat:] = agg_bf
    comb_pre = pre_ref[...] + dot(agg_bf, combw_ref[feat:, :])
    hidden = comb_pre * sigmoid(comb_pre)
    inv_norm = lax.rsqrt(jnp.mean(hidden * hidden, axis=1, keepdims=True) + eps)
    embed = (hidden * inv_norm).astype(BF16)

    own = rows(me * tgts, tgts)
    all_ref[own, :] = embed
    ring = Ring(grps, all_ref, tgts, ring_send, ring_recv)
    ring.begin()
    own_gain = gains_ref[own, :]
    own_query = (embed.astype(F32) * own_gain).astype(BF16)

    def score(block):
        at = rows(block * tgts, tgts)
        block_embed = all_ref[at, :]
        block_query = (block_embed.astype(F32) * gains_ref[at, :]).astype(BF16)
        query_ref[at, :] = block_query
        rt_ref[at, :] = dot_nt(block_embed, own_query) / feat
        ct_ref[at, :] = dot_nt(all_ref[own, :], block_query) / feat

    score(me)
    for hop in range(1, ring.hops + 1):
        ring.step(hop)
        ring.other(hop - 1)
        if hop < ring.hops:
            score(ring.origin(0, hop))
            score(ring.origin(1, hop))
        else:
            score(ring.origin(0, hop))
        for side in (0, 1) if hop > 1 else (0,):
            score(ring.origin(side, hop - 1) + 1 - 2 * ring.core)
    ring.other(ring.hops)
    score(ring.origin(0, ring.hops) + 1 - 2 * ring.core)

    scores = rt_ref[...]
    top = jnp.max(scores, axis=0, keepdims=True)
    terms = jnp.exp(scores - top)
    norm = jnp.sum(terms, axis=0, keepdims=True)
    own_stat = rows(me * 8, 8)
    stat_ref[own_stat, :] = jnp.concatenate(
        [jnp.broadcast_to(top, (4, LANES)), jnp.broadcast_to(norm, (4, LANES))], axis=0
    )
    stats = Stage(grps, me, lambda to: (node, to), lambda to: stat_ref.at[own_stat, :], stat_ref, 8, stat_send, stat_recv)
    stats.start()
    hit = jnp.where(iota((group, tgts), 0) == pos_ref[pl.ds(me, 1), :], 1.0, 0.0)
    picked = jnp.sum(scores * hit, axis=0, keepdims=True)
    loss_ref[...] = top + jnp.log(norm) - picked
    grad = ((terms / norm - hit) / group / feat).astype(BF16)
    query_grad = dot_tn(grad, all_ref[...])
    stats.arrive()

    def column(block, acc):
        at = rows(block * tgts, tgts)
        stat = stat_ref[rows(block * 8, 8), :]
        terms = jnp.exp(ct_ref[at, :] - stat[0:1, :]) / stat[4:5, :]
        mine = iota((tgts, LANES), 0) + me * tgts == pos_ref[pl.ds(block, 1), :]
        grad = ((terms - jnp.where(mine, 1.0, 0.0)) / group / feat).astype(BF16)
        return acc + dot(grad, query_ref[at, :])

    column_grad = lax.fori_loop(0, grps, column, jnp.zeros((tgts, feat), F32))
    embed_grad = query_grad * own_gain + column_grad
    logistic = sigmoid(comb_pre)
    inner = jnp.sum(hidden * embed_grad, axis=1, keepdims=True)
    cube = inv_norm * inv_norm * inv_norm
    hidden_grad = inv_norm * embed_grad - hidden * (cube * inner / feat)
    slope = logistic * (1.0 + comb_pre * (1.0 - logistic))
    pre_grad = (slope * hidden_grad).astype(BF16)
    agg = dot_nt(pre_grad, combw_ref[feat:, :]) / total

    agg_bf = agg.astype(BF16)
    for which, path in enumerate(paths):
        path.agg[rows(path.me2 * LANES, LANES), :] = agg_bf[:, which * half : which * half + half]
        path.agg_out.start()

    cols = feat // grps
    cpart_ref[:, : 2 * feat] = dot_tn(pre_grad, comb_in_ref[...]).astype(BF16)
    pick = ones_where(as_column(labels_ref[pl.ds(me, 1), :]) == lane)
    head = query_grad * embed.astype(F32)
    head_hi = head.astype(BF16)
    head_lo = (head - head_hi.astype(F32)).astype(BF16)
    cpart_ref[:, 2 * feat :] = (dot_tn(head_hi, pick) + dot_tn(head_lo, pick)).astype(BF16)
    comb_sum = Stage(
        grps, me, lambda to: (node, to), lambda to: cpart_ref.at[rows(to * cols, cols), :], cland_ref, cols, cpart_send, cpart_recv
    )
    comb_sum.start()
    comb_full = NodeSum(nodes, cpieces, cz_in, cmine, cy_in, cfull, (c0, c1, c2, c3, c4, c5))
    msg_full = NodeSum(nodes, mpieces, mz_in, mmine, my_in, mfull, (m0, m1, m2, m3, m4, m5))

    each_first(0, lambda path, which, step: path.spread(path.first(step), upper, lower))

    for path in paths:
        path.agg_out.arrive()

    def give(path, which, step):
        first = path.first(step)
        path.out2[rows(first * path.block, path.block), :] = dot(path.at[first], path.agg[...]).astype(BF16)
        path.rows_back.copy(first, path.me1).start()

    each_first(1, give)

    def slopes(tile, _):
        at = rows(tile * LANES, LANES)
        slope_ref[at, :] = silu_slope(slope_ref[at, :])
        return 0

    lax.fori_loop(0, pins // LANES, slopes, 0)
    for which, path in enumerate(paths):
        kept = dot(path.at[path.me1], path.agg[...]).astype(BF16)
        acc_ref[:, which * half : which * half + half] = dot(path.pt[path.me1], kept)

    def take(path, which, step):
        first = path.first(step)
        path.rows_back.copy(first, first).wait_recv()
        acc_ref[:, which * half : which * half + half] += dot(
            path.pt[first], path.in2[rows(first * path.block, path.block), :]
        )

    each_first(1, take)

    msg_grad = (slope_ref[...] * acc_ref[...]).astype(BF16)
    part = dot_tn(msg_grad, bf_ref[...]).astype(BF16)
    for g in range(grps):
        first = (g % 2) * half + (g // 2) * cols
        mpart_ref[first : first + cols, :] = part[g * cols : g * cols + cols, :]
    core, chip = lax.rem(me, 2), me // 2
    pair = pltpu.make_async_remote_copy(
        src_ref=mpart_ref.at[rows((1 - core) * half, half), :],
        dst_ref=pair_ref,
        send_sem=pair_send,
        recv_sem=pair_recv,
        device_id=(node, chip * 2 + 1 - core),
        device_id_type=MESH,
    )
    pair.start()
    comb_sum.arrive()
    comb_full.begin(comb_sum.total(cpart_ref[rows(me * cols, cols), :].astype(F32)))
    pair.wait_recv()
    mhalf_ref[...] = (mpart_ref[rows(core * half, half), :].astype(F32) + pair_ref[...].astype(F32)).astype(BF16)
    over_x = Stage(
        grps // 2, chip, lambda to: (node, to * 2 + core), lambda to: mhalf_ref.at[rows(to * cols, cols), :], mland_ref, cols, mx_send, mx_recv
    )
    over_x.start()
    comb_full.over_y()
    over_x.arrive()
    msg_full.begin(over_x.total(mhalf_ref[rows(chip * cols, cols), :].astype(F32)))
    comb_full.gather()
    msg_full.over_y()
    msg_full.gather()
    for path in paths:
        path.finish()
    ring.finish()
    stats.finish()
    comb_sum.finish()
    comb_full.end()
    comb_full.finish()
    pair.wait_send()
    over_x.finish()
    msg_full.end()
    msg_full.finish()


def outputs_kernel(loss_in, mfull, cfull, loss_ref, gmsg_ref, gcomb_ref, ghead_ref):
    loss_ref[...] = loss_in[...]
    gmsg_ref[...] = from_pieces(mfull, gmsg_ref.shape)
    cols, both = gcomb_ref.shape
    value = from_pieces(cfull, (cols, both + LANES))
    gcomb_ref[...] = value[:, :both]
    head = value[:, both:]
    if cols < LANES:
        head = jnp.concatenate([head, jnp.zeros((LANES - cols, LANES), F32)], axis=0)
    ghead_ref[...] = jnp.transpose(head)[: ghead_ref.shape[0], : ghead_ref.shape[1]]


def body(
    nodes, grps, nbr_feats, tgt_feats, msg_weight, comb_weight, head_gain, owners, serve_rows, importance,
    labels, positives,
):
    pins, feat = nbr_feats.shape
    tgts, tasks = tgt_feats.shape[0], head_gain.shape[0]
    group, half = tgts * grps, feat // 2
    cols, planes, chips = feat // grps, nodes // ROW, grps // 2
    hops, cap = chips // 2, serve_rows.shape[2]
    links = 2 * max(2 * hops - 1, 0)
    wide = 2 * feat + LANES

    def vm(kind, *shape):
        return pltpu.VMEM(shape, kind)

    def dma(*shape):
        return pltpu.SemaphoreType.DMA(shape)

    def per_of(width):
        return -(-(cols // 8 * (width // LANES)) // planes) * LANES

    def sum_scratch(width):
        per = per_of(width)
        piece = [vm(F32, planes * 8, per), vm(F32, planes * 8, per), vm(F32, 8, per), vm(F32, ROW * 8, per)]
        return piece + [dma(planes), dma(planes), dma(ROW), dma(ROW), dma(planes), dma(planes)]

    def path_scratch(firsts, seconds):
        block, tall = cap * seconds, seconds * LANES
        return [
            vm(I32, seconds * 16, LANES), vm(BF16, tall, LANES), vm(BF16, tall, LANES), vm(F32, LANES, tall), vm(F32, LANES, tall),
            vm(BF16, firsts, tall, block), vm(BF16, firsts, block, tall), vm(BF16, firsts, pins, block),
            vm(BF16, firsts * block, half), vm(BF16, firsts * block, half),
            vm(F32, tall, half), vm(BF16, tall, half), vm(BF16, tall, half), vm(BF16, tall, half),
            vm(BF16, firsts * block, half), vm(BF16, firsts * block, half),
        ]

    def path_sems(firsts, seconds):
        counts = [seconds, firsts, seconds, seconds, firsts]
        return [dma(count) for count in counts for _ in range(2)]

    scratch = [
        vm(BF16, pins, half), vm(BF16, pins, half), vm(BF16, pins, feat), vm(F32, pins, feat), vm(F32, LANES, LANES), vm(F32, LANES, LANES),
        path_scratch(ROW, planes), path_scratch(planes, ROW), path_sems(ROW, planes), path_sems(planes, ROW),
        vm(BF16, tgts, 2 * feat), vm(F32, tgts, feat),
        vm(BF16, group, feat), vm(BF16, group, feat), vm(F32, group, feat), vm(F32, group, tgts), vm(F32, group, tgts),
        dma(2 * links + 2), dma(2 * links + 2), vm(F32, grps * 8, LANES), dma(grps), dma(grps),
        vm(F32, pins, feat),
        vm(BF16, feat, wide), vm(BF16, feat, wide), dma(grps), dma(grps), *sum_scratch(wide),
        vm(BF16, feat, feat), vm(BF16, half, feat), pltpu.SemaphoreType.DMA, pltpu.SemaphoreType.DMA,
        vm(BF16, half, feat), vm(BF16, half, feat), dma(chips), dma(chips), *sum_scratch(feat),
    ]
    args = (
        nbr_feats, tgt_feats, msg_weight, comb_weight, head_gain, serve_rows[0].T, owners.T, importance.T,
        labels.reshape(grps, tgts), positives.reshape(grps, tgts),
    )
    whole = pl.BlockSpec(memory_space=pltpu.VMEM)
    outs = [(1, tgts), (planes * 8, per_of(feat)), (planes * 8, per_of(wide))]
    sums = pl.pallas_call(
        functools.partial(tower_kernel, nodes, grps),
        name="tower",
        out_shape=[jax.ShapeDtypeStruct(shape, F32) for shape in outs],
        in_specs=[whole] * len(args),
        out_specs=[whole] * len(outs),
        scratch_shapes=scratch,
        compiler_params=pltpu.CompilerParams(
            collective_id=0, has_side_effects=True, vmem_limit_bytes=60 * 2**20
        ),
    )(*args)
    outs = [(1, tgts), (cols, feat), (cols, 2 * feat), (tasks, cols)]
    loss, grad_msg, grad_comb, grad_head = pl.pallas_call(
        outputs_kernel,
        name="outputs",
        out_shape=[jax.ShapeDtypeStruct(shape, F32) for shape in outs],
        in_specs=[whole] * len(sums),
        out_specs=[whole] * len(outs),
    )(*sums)
    return loss.reshape(tgts), grad_msg.T, grad_comb.T, grad_head


def solution(mesh):
    placed = (
        P(("node", "grp"), None),
        P(("node", "grp"), None),
        P(),
        P(),
        P(),
        P(("node", "grp"), None),
        P(("node", "grp"), None, None),
        P(("node", "grp"), None),
        P("node"),
        P("node"),
    )
    return jax.shard_map(
        functools.partial(body, mesh.shape["node"], mesh.shape["grp"]),
        mesh=mesh,
        in_specs=placed,
        out_specs=(P(("node", "grp")), P(None, "grp"), P(None, "grp"), P(None, "grp")),
        check_vma=False,
    )
```

```python
import functools

import jax
import jax.numpy as jnp
from jax import lax
from jax.experimental import pallas as pl
from jax.experimental.pallas import tpu as pltpu
from jax.sharding import PartitionSpec as P

MESH = pl.DeviceIdType.MESH
F32, BF16, I32 = jnp.float32, jnp.bfloat16, jnp.int32
eps = 1e-05
LANES = 128
ROW = 8


def dot(left, right):
    return jnp.dot(left, right, preferred_element_type=F32)


def dot_nt(left, right):
    return lax.dot_general(left, right, (((1,), (1,)), ((), ())), preferred_element_type=F32)


def dot_tn(left, right):
    return lax.dot_general(left, right, (((0,), (0,)), ((), ())), preferred_element_type=F32)


def iota(shape, dim):
    return lax.broadcasted_iota(I32, shape, dim)


def ones_where(mask):
    return jnp.where(mask, 1.0, 0.0).astype(BF16)


def low(index, count):
    return index & (count - 1)


def high(index, count):
    return lax.shift_right_logical(index, jnp.full(index.shape, count.bit_length() - 1, I32))


def sigmoid(value):
    return 1.0 / (1.0 + jnp.exp(-value))


def silu_slope(value):
    logistic = sigmoid(value)
    return logistic * (1.0 + value * (1.0 - logistic))


def rows(start, size):
    return pl.ds(pl.multiple_of(start, size), size)


def as_column(row):
    return jnp.transpose(jnp.broadcast_to(row, (LANES, LANES)))


def greet(nodes, grps):
    node, grp = lax.axis_index("node"), lax.axis_index("grp")
    barrier = pltpu.get_barrier_semaphore()

    def hello_node(step, _):
        peer = (lax.rem(node + step, nodes), grp)
        pl.semaphore_signal(barrier, inc=1, device_id=peer, device_id_type=MESH)
        return 0

    def hello_grp(step, _):
        peer = (node, lax.rem(grp + step, grps))
        pl.semaphore_signal(barrier, inc=1, device_id=peer, device_id_type=MESH)
        return 0

    lax.fori_loop(1, nodes, hello_node, 0)
    lax.fori_loop(1, grps, hello_grp, 0)
    return lambda: pl.semaphore_wait(barrier, nodes + grps - 2)


def offset(step, count):
    return lax.rem(jnp.where(lax.rem(step, 2) == 1, (step + 1) // 2, count - step // 2), count)


class Stage:
    def __init__(self, count, me, peer, source, landing, size, send_sem, recv_sem):
        self.count, self.me, self.peer, self.source = count, me, peer, source
        self.landing, self.size, self.send_sem, self.recv_sem = landing, size, send_sem, recv_sem

    def copy(self, to, place):
        return pltpu.make_async_remote_copy(
            src_ref=self.source(to),
            dst_ref=self.landing.at[rows(place * self.size, self.size), :],
            send_sem=self.send_sem.at[to],
            recv_sem=self.recv_sem.at[place],
            device_id=self.peer(to),
            device_id_type=MESH,
        )

    def each(self, act):
        def step(i, _):
            act(lax.rem(self.me + offset(i, self.count), self.count))
            return 0

        lax.fori_loop(1, self.count, step, 0)

    def start(self):
        self.each(lambda to: self.copy(to, self.me).start())

    def arrive(self):
        self.each(lambda source: self.copy(source, source).wait_recv())

    def finish(self):
        self.each(lambda to: self.copy(to, self.me).wait_send())

    def total(self, own):
        def add(i, acc):
            source = lax.rem(self.me + i, self.count)
            return acc + self.landing[rows(source * self.size, self.size), :].astype(F32)

        return lax.fori_loop(1, self.count, add, own)


def to_pieces(value, ref):
    per = ref.shape[1] // LANES
    wide = value.shape[1] // LANES
    for k in range(value.shape[0] // 8 * wide):
        r, c = divmod(k, wide)
        piece, place = divmod(k, per)
        ref[piece * 8 : piece * 8 + 8, place * LANES : place * LANES + LANES] = value[
            r * 8 : r * 8 + 8, c * LANES : c * LANES + LANES
        ]


def from_pieces(ref, shape):
    per = ref.shape[1] // LANES
    wide = shape[1] // LANES
    bands = []
    for r in range(shape[0] // 8):
        band = []
        for c in range(wide):
            piece, place = divmod(r * wide + c, per)
            band.append(ref[piece * 8 : piece * 8 + 8, place * LANES : place * LANES + LANES])
        bands.append(jnp.concatenate(band, axis=1))
    return jnp.concatenate(bands, axis=0)


class Path:
    def __init__(self, nodes, y_first, cap, refs, sems):
        node, self.grp = lax.axis_index("node"), lax.axis_index("grp")
        planes = nodes // ROW
        z, y = node // ROW, lax.rem(node, ROW)
        self.y_first = y_first
        self.firsts, self.seconds = (ROW, planes) if y_first else (planes, ROW)
        self.me1, self.me2 = (y, z) if y_first else (z, y)
        self.block = cap * self.seconds
        (self.tab, self.ws, self.es, self.wt, self.et, self.a, self.at, self.pt, self.out, self.inn, self.sums, self.sent, self.land,
         self.agg, self.out2, self.in2, self.code) = refs
        block, me1, me2 = self.block, self.me1, self.me2
        firsts, seconds, peer1, peer2 = self.firsts, self.seconds, self.peer1, self.peer2

        def own_tab(to):
            return self.tab.at[rows(me2 * 16, 16), :]

        def own_agg(to):
            return self.agg.at[rows(me2 * LANES, LANES), :]

        self.tables = Stage(seconds, me2, peer2, own_tab, self.tab, 16, sems[0], sems[1])
        self.rows_out = Stage(firsts, me1, peer1, lambda to: self.out.at[rows(to * block, block), :], self.inn, block, sems[2], sems[3])
        self.sums_out = Stage(seconds, me2, peer2, lambda to: self.sent.at[rows(to * LANES, LANES), :], self.land, LANES, sems[4], sems[5])
        self.agg_out = Stage(seconds, me2, peer2, own_agg, self.agg, LANES, sems[6], sems[7])
        self.rows_back = Stage(firsts, me1, peer1, lambda to: self.out2.at[rows(to * block, block), :], self.in2, block, sems[8], sems[9])

    def node_of(self, first, second):
        return second * ROW + first if self.y_first else first * ROW + second

    def peer1(self, to):
        return (self.node_of(to, self.me2), self.grp)

    def peer2(self, to):
        return (self.node_of(self.me1, to), self.grp)

    def first(self, step):
        return lax.rem(self.me1 + offset(step, self.firsts), self.firsts)

    def put_tables(self, owners, weights):
        self.tab[rows(self.me2 * 16, 8), :] = owners
        self.tab[rows(self.me2 * 16 + 8, 8), :] = weights

    def key_column(self, first, upper, lower):
        sub, lane = iota((self.block, LANES), 0), iota((self.block, LANES), 1)
        pick = ones_where(lane == self.node_of(first, low(sub, self.seconds)))
        listed = dot_nt(pick, upper) * 2.0 + dot_nt(pick, lower)
        return jnp.sum(jnp.where(lane == high(sub, self.seconds), listed, 0.0), axis=1, keepdims=True)

    def key_row(self, first, upper, lower):
        sub, lane = iota((self.block, LANES), 0), iota((self.block, LANES), 1)
        pick = ones_where(lane == self.node_of(first, low(sub, self.seconds)))
        listed = dot_nt(upper, pick) * 2.0 + dot_nt(lower, pick)
        sub, lane = iota((LANES, self.block), 0), iota((LANES, self.block), 1)
        return jnp.sum(jnp.where(sub == high(lane, self.seconds), listed, 0.0), axis=0, keepdims=True)

    def serve(self, first, upper, lower, messages):
        key = self.key_column(first, upper, lower)
        pick = ones_where(key == iota((self.block, messages.shape[0]), 1).astype(F32))
        self.out[rows(first * self.block, self.block), :] = dot(pick, messages[...]).astype(BF16)

    def keep(self, out, inn):
        own = rows(self.me1 * self.block, self.block)
        inn[own, :] = out[own, :]

    def read_tables(self, above):
        sub = iota((LANES, LANES), 0)

        def read(second, _):
            hits = jnp.zeros((LANES, LANES), F32)
            weights = jnp.zeros((LANES, LANES), F32)
            for k in range(8):
                hit = self.tab[pl.ds(second * 16 + k, 1), :] == sub
                hits = hits + jnp.where(hit, 1.0, 0.0)
                weights = weights + jnp.where(hit, self.tab[pl.ds(second * 16 + 8 + k, 1), :].astype(F32), 0.0)
            earlier = dot(hits.astype(BF16), above)
            at = rows(second * LANES, LANES)
            self.wt[:, at] = weights
            self.et[:, at] = earlier
            self.ws[at, :] = jnp.transpose(weights).astype(BF16)
            self.es[at, :] = jnp.transpose(earlier).astype(BF16)
            return 0

        lax.fori_loop(0, self.seconds, read, 0)

    def weigh(self, first):
        owner = self.node_of(first, self.me2)
        spread = ones_where(iota((LANES, self.block), 0) == owner)
        weight, slot = dot(self.ws[...], spread), dot(self.es[...], spread)
        lane = iota((8, self.block), 1)
        for second in range(self.seconds):
            at = slice(second * LANES, second * LANES + LANES)
            code = jnp.where(low(lane, self.seconds) == second, high(lane, self.seconds), -1).astype(F32)[:1]
            self.a[first, at, :] = jnp.where(slot[at] == code, weight[at], 0.0).astype(BF16)

    def number(self):
        sub = iota((self.block, LANES), 0)
        for second in range(self.seconds):
            self.code[second] = jnp.where(low(sub, self.seconds) == second, high(sub, self.seconds), -1).astype(F32)

    def weigh_back(self, first):
        owner = self.node_of(first, self.me2)
        weight, slot = self.wt[pl.ds(owner, 1), :], self.et[pl.ds(owner, 1), :]
        for second in range(self.seconds):
            at = slice(second * LANES, second * LANES + LANES)
            self.at[first, :, at] = jnp.where(slot[:, at] == self.code[second], weight[:, at], 0.0).astype(BF16)

    def spread(self, first, upper, lower):
        key = self.key_row(first, upper, lower)
        self.pt[first] = ones_where(iota((self.pt.shape[1], self.block), 0).astype(F32) == key)

    def finish(self):
        for stage in (self.tables, self.rows_out, self.sums_out, self.agg_out, self.rows_back):
            stage.finish()


class NodeSum:
    def __init__(self, nodes, pieces, z_in, mine, y_in, full, sems):
        node, grp = lax.axis_index("node"), lax.axis_index("grp")
        planes = nodes // ROW
        self.z, self.y = node // ROW, lax.rem(node, ROW)
        z, y = self.z, self.y
        self.pieces, self.mine, self.y_in, self.full = pieces, mine, y_in, full

        def z_peer(to):
            return (to * ROW + y, grp)

        def y_peer(to):
            return (z * ROW + to, grp)

        self.first = Stage(planes, z, z_peer, lambda to: pieces.at[rows(to * 8, 8), :], z_in, 8, sems[0], sems[1])
        self.second = Stage(ROW, y, y_peer, lambda to: mine, y_in, 8, sems[2], sems[3])
        self.third = Stage(planes, z, z_peer, lambda to: full.at[rows(z * 8, 8), :], full, 8, sems[4], sems[5])

    def begin(self, value):
        if self.pieces.shape[0] * self.pieces.shape[1] > value.shape[0] * value.shape[1]:
            self.pieces[...] = jnp.zeros_like(self.pieces)
        to_pieces(value, self.pieces)
        self.first.start()

    def over_y(self):
        self.first.arrive()
        own = self.first.total(self.pieces[rows(self.z * 8, 8), :])
        self.mine[...] = own
        self.y_in[rows(self.y * 8, 8), :] = own
        self.second.start()

    def gather(self):
        self.second.arrive()
        total = self.y_in[:8, :]
        for k in range(1, ROW):
            total = total + self.y_in[k * 8 : k * 8 + 8, :]
        self.full[rows(self.z * 8, 8), :] = total
        self.third.start()

    def end(self):
        self.third.arrive()

    def finish(self):
        for stage in (self.first, self.second, self.third):
            stage.finish()


class Ring:
    def __init__(self, grps, all_ref, size, send_sem, recv_sem):
        node, me = lax.axis_index("node"), lax.axis_index("grp")
        self.node, self.me, self.all_ref, self.size = node, me, all_ref, size
        self.send_sem, self.recv_sem = send_sem, recv_sem
        self.chips, self.core, self.chip = grps // 2, lax.rem(me, 2), me // 2
        self.hops = self.chips // 2
        self.index, self.started = {}, []
        for side in (0, 1):
            for hop in range(1, self.hops + 1):
                for piece in (0, 1):
                    if hop < self.hops or piece == side:
                        self.index["link", side, hop, piece] = len(self.index)
        for key in list(self.index):
            self.index[("core",) + key[1:]] = len(self.index)
        for piece in (0, 1):
            self.index["core", 0, 0, piece] = len(self.index)

    def at_chip(self, steps):
        return lax.rem(self.chip + self.chips + steps, self.chips) * 2 + self.core

    def origin(self, side, hop):
        return self.at_chip(-hop if side == 0 else hop)

    def copy(self, key):
        kind, side, hop, piece = key
        origin = self.origin(side, hop - 1 if kind == "link" else hop)
        half = self.size // 2
        at = rows(origin * self.size + piece * half, half)
        to = self.at_chip(1 if side == 0 else -1) if kind == "link" else self.chip * 2 + 1 - self.core
        return pltpu.make_async_remote_copy(
            src_ref=self.all_ref.at[at, :],
            dst_ref=self.all_ref.at[at, :],
            send_sem=self.send_sem.at[self.index[key]],
            recv_sem=self.recv_sem.at[self.index[key]],
            device_id=(self.node, to),
            device_id_type=MESH,
        )

    def start(self, *key):
        if key in self.index:
            self.copy(key).start()
            self.started.append(key)

    def arrive(self, *key):
        if key in self.index:
            self.copy(key).wait_recv()

    def begin(self):
        for piece in (0, 1):
            for side in (0, 1):
                self.start("link", side, 1, piece ^ side)
        for piece in (0, 1):
            self.start("core", 0, 0, piece)

    def step(self, hop):
        for piece in (0, 1):
            for side in (0, 1):
                key = (side, hop, piece ^ side)
                self.arrive("link", *key)
                self.start("link", side, hop + 1, piece ^ side)
                if ("link", *key) in self.index:
                    self.start("core", *key)

    def other(self, hop):
        for side in (0, 1):
            for piece in (0, 1):
                if hop or side == 0:
                    self.arrive("core", side, hop, piece)

    def finish(self):
        for key in self.started:
            self.copy(key).wait_send()


def tower_kernel(
    nodes, grps, nbr_ref, tgt_ref, msgw_ref, combw_ref, gain_ref, served_ref, owners_ref, weight_ref, labels_ref, pos_ref,
    loss_ref, mfull, cfull,
    msg0_ref, msg1_ref, bf_ref, slope_ref, upper_ref, lower_ref, path0, path1, sems0, sems1,
    comb_in_ref, pre_ref,
    all_ref, query_ref, gains_ref, rt_ref, ct_ref, gct_ref, ring_send, ring_recv, stat_ref, stat_send, stat_recv,
    acc_ref,
    cpart_ref, cland_ref, cpart_send, cpart_recv, cpieces, cz_in, cmine, cy_in, c0, c1, c2, c3, c4, c5,
    mpart_ref, pair_ref, pair_send, pair_recv, mhalf_ref, mland_ref, mx_send, mx_recv,
    mpieces, mz_in, mmine, my_in, m0, m1, m2, m3, m4, m5,
):
    ready = greet(nodes, grps)
    node, me = lax.axis_index("node"), lax.axis_index("grp")
    feat, tgts, pins = msgw_ref.shape[0], tgt_ref.shape[0], nbr_ref.shape[0]
    half, group = feat // 2, tgts * grps
    lane = iota((LANES, LANES), 1)
    sub = iota((LANES, LANES), 0)
    cap = served_ref.shape[0]
    paths = [Path(nodes, True, cap, path0, sems0), Path(nodes, False, cap, path1, sems1)]
    longest = max(path.firsts for path in paths)
    halves = (msg0_ref, msg1_ref)

    def each_first(first, act):
        def turn(step, _):
            for which, path in enumerate(paths):
                if path.firsts == longest:
                    act(path, which, step)
                else:
                    pl.when(step < path.firsts)(functools.partial(act, path, which, step))
            return 0

        lax.fori_loop(first, longest, turn, 0)

    def message(tile, _):
        at = rows(tile * LANES, LANES)
        nbr = nbr_ref[at, :].astype(BF16)
        bf_ref[at, :] = nbr
        pre = dot(nbr, msgw_ref[...])
        slope_ref[at, :] = pre
        msg = (pre * sigmoid(pre)).astype(BF16)
        msg0_ref[at, :] = msg[:, :half]
        msg1_ref[at, :] = msg[:, half:]
        return 0

    lax.fori_loop(0, pins // LANES, message, 0)
    upper_ref[...] = jnp.zeros_like(upper_ref)
    lower_ref[...] = jnp.zeros_like(lower_ref)
    served = served_ref[...]
    upper_ref[:cap, : served.shape[1]] = (served // 2).astype(F32)
    lower_ref[:cap, : served.shape[1]] = (served % 2).astype(F32)
    upper, lower = upper_ref[...].astype(BF16), lower_ref[...].astype(BF16)
    for path in paths:
        path.put_tables(owners_ref[...], weight_ref[...])
    ready()
    for path in paths:
        path.tables.start()

    def serve(path, which, step):
        first = path.first(step)
        path.serve(first, upper, lower, halves[which])
        path.rows_out.copy(first, path.me1).start()

    each_first(1, serve)
    for path, messages in zip(paths, halves):
        path.serve(path.me1, upper, lower, messages)
        path.keep(path.out, path.inn)

    above = ones_where(sub < lane)
    for path in paths:
        path.tables.arrive()
        path.read_tables(above)
    each_first(0, lambda path, which, step: path.weigh(path.first(step)))
    for path in paths:
        path.sums[...] = dot(path.a[path.me1], path.inn[rows(path.me1 * path.block, path.block), :])
    own_path = paths[0]
    total = jnp.sum(own_path.ws[rows(own_path.me2 * LANES, LANES), :].astype(F32), axis=1, keepdims=True)
    tgt_bf = tgt_ref[...].astype(BF16)
    comb_in_ref[:, :feat] = tgt_bf
    pre_ref[...] = dot(tgt_bf, combw_ref[:feat, :])

    def collect(path, which, step):
        first = path.first(step)
        path.rows_out.copy(first, first).wait_recv()
        path.sums[...] += dot(path.a[first], path.inn[rows(first * path.block, path.block), :])

    each_first(1, collect)
    for path in paths:
        path.sent[...] = path.sums[...].astype(BF16)
        path.sums_out.start()

    for path in paths:
        path.number()
    each_first(0, lambda path, which, step: path.weigh_back(path.first(step)))
    gain = gain_ref[...]
    gain_hi = gain.astype(BF16).astype(F32)
    gain_mid = (gain - gain_hi).astype(BF16).astype(F32)
    gain_lo = gain - gain_hi - gain_mid
    tasks = gain.shape[0]
    gain3 = jnp.concatenate(
        [gain_hi, gain_mid, gain_lo, jnp.zeros((LANES - 3 * tasks, feat), F32)], axis=0
    ).astype(BF16)

    task = lane % tasks

    def gains(block, _):
        label = as_column(labels_ref[pl.ds(block, 1), :])
        pick = ones_where((label == task) & (lane < 3 * tasks))
        gains_ref[rows(block * tgts, tgts), :] = dot(pick, gain3)
        return 0

    lax.fori_loop(0, grps, gains, 0)
    sums = []
    for path in paths:
        path.sums_out.arrive()
        sums.append(path.sums_out.total(path.sums[rows(path.me2 * LANES, LANES), :]))
    agg_bf = (jnp.concatenate(sums, axis=1) / total).astype(BF16)
    comb_in_ref[:, feat:] = agg_bf
    comb_pre = pre_ref[...] + dot(agg_bf, combw_ref[feat:, :])
    hidden = comb_pre * sigmoid(comb_pre)
    inv_norm = lax.rsqrt(jnp.mean(hidden * hidden, axis=1, keepdims=True) + eps)
    embed = (hidden * inv_norm).astype(BF16)

    own = rows(me * tgts, tgts)
    all_ref[own, :] = embed
    ring = Ring(grps, all_ref, tgts, ring_send, ring_recv)
    ring.begin()
    own_gain = gains_ref[own, :]
    own_query = (embed.astype(F32) * own_gain).astype(BF16)

    def score(block):
        at = rows(block * tgts, tgts)
        block_embed = all_ref[at, :]
        block_query = (block_embed.astype(F32) * gains_ref[at, :]).astype(BF16)
        query_ref[at, :] = block_query
        rt_ref[at, :] = dot_nt(block_embed, own_query) * (1.0 / feat)
        ct_ref[at, :] = dot_nt(all_ref[own, :], block_query) * (1.0 / feat)

    score(me)
    for hop in range(1, ring.hops + 1):
        ring.step(hop)
        ring.other(hop - 1)
        if hop < ring.hops:
            score(ring.origin(0, hop))
            score(ring.origin(1, hop))
        else:
            score(ring.origin(0, hop))
        for side in (0, 1) if hop > 1 else (0,):
            score(ring.origin(side, hop - 1) + 1 - 2 * ring.core)
    ring.other(ring.hops)
    score(ring.origin(0, ring.hops) + 1 - 2 * ring.core)

    scores = rt_ref[...]
    top = jnp.max(scores, axis=0, keepdims=True)
    terms = jnp.exp(scores - top)
    norm = jnp.sum(terms, axis=0, keepdims=True)
    own_stat = rows(me * 8, 8)
    stat_ref[own_stat, :] = jnp.concatenate(
        [jnp.broadcast_to(top, (4, LANES)), jnp.broadcast_to(norm, (4, LANES))], axis=0
    )
    stats = Stage(grps, me, lambda to: (node, to), lambda to: stat_ref.at[own_stat, :], stat_ref, 8, stat_send, stat_recv)
    stats.start()
    hit = jnp.where(iota((group, tgts), 0) == pos_ref[pl.ds(me, 1), :], 1.0, 0.0)
    picked = jnp.sum(scores * hit, axis=0, keepdims=True)
    loss_ref[...] = top + jnp.log(norm) - picked
    grad = ((terms * (1.0 / norm) - hit) * (1.0 / group / feat)).astype(BF16)
    query_grad = dot_tn(grad, all_ref[...])
    stats.arrive()

    place = sub + me * tgts

    def column(block, _):
        stat = stat_ref[rows(block * 8, 8), :]
        terms = jnp.exp(ct_ref[rows(block * tgts, tgts), :] - stat[0:1, :]) * (1.0 / stat[4:5, :])
        hit = jnp.where(place == pos_ref[pl.ds(block, 1), :], 1.0, 0.0)
        gct_ref[:, rows(block * tgts, tgts)] = ((terms - hit) * (1.0 / group / feat)).astype(BF16)
        return 0

    lax.fori_loop(0, grps, column, 0, unroll=4)
    column_grad = dot(gct_ref[...], query_ref[...])
    embed_grad = query_grad * own_gain + column_grad
    logistic = sigmoid(comb_pre)
    inner = jnp.sum(hidden * embed_grad, axis=1, keepdims=True)
    cube = inv_norm * inv_norm * inv_norm
    hidden_grad = inv_norm * embed_grad - hidden * (cube * inner / feat)
    slope = logistic * (1.0 + comb_pre * (1.0 - logistic))
    pre_grad = (slope * hidden_grad).astype(BF16)
    agg = dot_nt(pre_grad, combw_ref[feat:, :]) / total

    agg_bf = agg.astype(BF16)
    for which, path in enumerate(paths):
        path.agg[rows(path.me2 * LANES, LANES), :] = agg_bf[:, which * half : which * half + half]
        path.agg_out.start()

    cols = feat // grps
    cpart_ref[:, : 2 * feat] = dot_tn(pre_grad, comb_in_ref[...]).astype(BF16)
    pick = ones_where(as_column(labels_ref[pl.ds(me, 1), :]) == lane)
    head = query_grad * embed.astype(F32)
    head_hi = head.astype(BF16)
    head_lo = (head - head_hi.astype(F32)).astype(BF16)
    cpart_ref[:, 2 * feat :] = (dot_tn(head_hi, pick) + dot_tn(head_lo, pick)).astype(BF16)
    comb_sum = Stage(
        grps, me, lambda to: (node, to), lambda to: cpart_ref.at[rows(to * cols, cols), :], cland_ref, cols, cpart_send, cpart_recv
    )
    comb_sum.start()
    comb_full = NodeSum(nodes, cpieces, cz_in, cmine, cy_in, cfull, (c0, c1, c2, c3, c4, c5))
    msg_full = NodeSum(nodes, mpieces, mz_in, mmine, my_in, mfull, (m0, m1, m2, m3, m4, m5))

    each_first(0, lambda path, which, step: path.spread(path.first(step), upper, lower))

    for path in paths:
        path.agg_out.arrive()

    def give(path, which, step):
        first = path.first(step)
        path.out2[rows(first * path.block, path.block), :] = dot(path.at[first], path.agg[...]).astype(BF16)
        path.rows_back.copy(first, path.me1).start()

    each_first(1, give)

    def slopes(tile, _):
        at = rows(tile * LANES, LANES)
        slope_ref[at, :] = silu_slope(slope_ref[at, :])
        return 0

    lax.fori_loop(0, pins // LANES, slopes, 0)
    for which, path in enumerate(paths):
        kept = dot(path.at[path.me1], path.agg[...]).astype(BF16)
        acc_ref[:, which * half : which * half + half] = dot(path.pt[path.me1], kept)

    def take(path, which, step):
        first = path.first(step)
        path.rows_back.copy(first, first).wait_recv()
        acc_ref[:, which * half : which * half + half] += dot(
            path.pt[first], path.in2[rows(first * path.block, path.block), :]
        )

    each_first(1, take)

    msg_grad = (slope_ref[...] * acc_ref[...]).astype(BF16)
    part = dot_tn(msg_grad, bf_ref[...]).astype(BF16)
    for g in range(grps):
        first = (g % 2) * half + (g // 2) * cols
        mpart_ref[first : first + cols, :] = part[g * cols : g * cols + cols, :]
    core, chip = lax.rem(me, 2), me // 2
    pair = pltpu.make_async_remote_copy(
        src_ref=mpart_ref.at[rows((1 - core) * half, half), :],
        dst_ref=pair_ref,
        send_sem=pair_send,
        recv_sem=pair_recv,
        device_id=(node, chip * 2 + 1 - core),
        device_id_type=MESH,
    )
    pair.start()
    comb_sum.arrive()
    comb_full.begin(comb_sum.total(cpart_ref[rows(me * cols, cols), :].astype(F32)))
    pair.wait_recv()
    mhalf_ref[...] = (mpart_ref[rows(core * half, half), :].astype(F32) + pair_ref[...].astype(F32)).astype(BF16)
    over_x = Stage(
        grps // 2, chip, lambda to: (node, to * 2 + core), lambda to: mhalf_ref.at[rows(to * cols, cols), :], mland_ref, cols, mx_send, mx_recv
    )
    over_x.start()
    comb_full.over_y()
    over_x.arrive()
    msg_full.begin(over_x.total(mhalf_ref[rows(chip * cols, cols), :].astype(F32)))
    comb_full.gather()
    msg_full.over_y()
    msg_full.gather()
    for path in paths:
        path.finish()
    ring.finish()
    stats.finish()
    comb_sum.finish()
    comb_full.end()
    comb_full.finish()
    pair.wait_send()
    over_x.finish()
    msg_full.end()
    msg_full.finish()


def outputs_kernel(loss_in, mfull, cfull, loss_ref, gmsg_ref, gcomb_ref, ghead_ref):
    loss_ref[...] = loss_in[...]
    gmsg_ref[...] = from_pieces(mfull, gmsg_ref.shape)
    cols, both = gcomb_ref.shape
    value = from_pieces(cfull, (cols, both + LANES))
    gcomb_ref[...] = value[:, :both]
    head = value[:, both:]
    if cols < LANES:
        head = jnp.concatenate([head, jnp.zeros((LANES - cols, LANES), F32)], axis=0)
    ghead_ref[...] = jnp.transpose(head)[: ghead_ref.shape[0], : ghead_ref.shape[1]]


def body(
    nodes, grps, nbr_feats, tgt_feats, msg_weight, comb_weight, head_gain, owners, serve_rows, importance,
    labels, positives,
):
    pins, feat = nbr_feats.shape
    tgts, tasks = tgt_feats.shape[0], head_gain.shape[0]
    group, half = tgts * grps, feat // 2
    cols, planes, chips = feat // grps, nodes // ROW, grps // 2
    hops, cap = chips // 2, serve_rows.shape[2]
    links = 2 * max(2 * hops - 1, 0)
    wide = 2 * feat + LANES

    def vm(kind, *shape):
        return pltpu.VMEM(shape, kind)

    def dma(*shape):
        return pltpu.SemaphoreType.DMA(shape)

    def per_of(width):
        return -(-(cols // 8 * (width // LANES)) // planes) * LANES

    def sum_scratch(width):
        per = per_of(width)
        piece = [vm(F32, planes * 8, per), vm(F32, planes * 8, per), vm(F32, 8, per), vm(F32, ROW * 8, per)]
        return piece + [dma(planes), dma(planes), dma(ROW), dma(ROW), dma(planes), dma(planes)]

    def path_scratch(firsts, seconds):
        block, tall = cap * seconds, seconds * LANES
        return [
            vm(I32, seconds * 16, LANES), vm(BF16, tall, LANES), vm(BF16, tall, LANES), vm(F32, LANES, tall), vm(F32, LANES, tall),
            vm(BF16, firsts, tall, block), vm(BF16, firsts, block, tall), vm(BF16, firsts, pins, block),
            vm(BF16, firsts * block, half), vm(BF16, firsts * block, half),
            vm(F32, tall, half), vm(BF16, tall, half), vm(BF16, tall, half), vm(BF16, tall, half),
            vm(BF16, firsts * block, half), vm(BF16, firsts * block, half), vm(F32, seconds, block, LANES),
        ]

    def path_sems(firsts, seconds):
        counts = [seconds, firsts, seconds, seconds, firsts]
        return [dma(count) for count in counts for _ in range(2)]

    scratch = [
        vm(BF16, pins, half), vm(BF16, pins, half), vm(BF16, pins, feat), vm(F32, pins, feat), vm(F32, LANES, LANES), vm(F32, LANES, LANES),
        path_scratch(ROW, planes), path_scratch(planes, ROW), path_sems(ROW, planes), path_sems(planes, ROW),
        vm(BF16, tgts, 2 * feat), vm(F32, tgts, feat),
        vm(BF16, group, feat), vm(BF16, group, feat), vm(F32, group, feat), vm(F32, group, tgts), vm(F32, group, tgts), vm(BF16, tgts, group),
        dma(2 * links + 2), dma(2 * links + 2), vm(F32, grps * 8, LANES), dma(grps), dma(grps),
        vm(F32, pins, feat),
        vm(BF16, feat, wide), vm(BF16, feat, wide), dma(grps), dma(grps), *sum_scratch(wide),
        vm(BF16, feat, feat), vm(BF16, half, feat), pltpu.SemaphoreType.DMA, pltpu.SemaphoreType.DMA,
        vm(BF16, half, feat), vm(BF16, half, feat), dma(chips), dma(chips), *sum_scratch(feat),
    ]
    args = (
        nbr_feats, tgt_feats, msg_weight, comb_weight, head_gain, serve_rows[0].T, owners.T, importance.T,
        labels.reshape(grps, tgts), positives.reshape(grps, tgts),
    )
    whole = pl.BlockSpec(memory_space=pltpu.VMEM)
    outs = [(1, tgts), (planes * 8, per_of(feat)), (planes * 8, per_of(wide))]
    sums = pl.pallas_call(
        functools.partial(tower_kernel, nodes, grps),
        name="tower",
        out_shape=[jax.ShapeDtypeStruct(shape, F32) for shape in outs],
        in_specs=[whole] * len(args),
        out_specs=[whole] * len(outs),
        scratch_shapes=scratch,
        compiler_params=pltpu.CompilerParams(
            collective_id=0, has_side_effects=True, vmem_limit_bytes=60 * 2**20
        ),
    )(*args)
    outs = [(1, tgts), (cols, feat), (cols, 2 * feat), (tasks, cols)]
    loss, grad_msg, grad_comb, grad_head = pl.pallas_call(
        outputs_kernel,
        name="outputs",
        out_shape=[jax.ShapeDtypeStruct(shape, F32) for shape in outs],
        in_specs=[whole] * len(sums),
        out_specs=[whole] * len(outs),
    )(*sums)
    return loss.reshape(tgts), grad_msg.T, grad_comb.T, grad_head


def solution(mesh):
    placed = (
        P(("node", "grp"), None),
        P(("node", "grp"), None),
        P(),
        P(),
        P(),
        P(("node", "grp"), None),
        P(("node", "grp"), None, None),
        P(("node", "grp"), None),
        P("node"),
        P("node"),
    )
    return jax.shard_map(
        functools.partial(body, mesh.shape["node"], mesh.shape["grp"]),
        mesh=mesh,
        in_specs=placed,
        out_specs=(P(("node", "grp")), P(None, "grp"), P(None, "grp"), P(None, "grp")),
        check_vma=False,
    )
```

```python
import functools

import jax
import jax.numpy as jnp
from jax import lax
from jax.experimental import pallas as pl
from jax.experimental.pallas import tpu as pltpu
from jax.sharding import PartitionSpec as P

MESH = pl.DeviceIdType.MESH
F32, BF16, I32 = jnp.float32, jnp.bfloat16, jnp.int32
eps = 1e-05
LANES = 128
ROW = 8


def dot(left, right):
    return jnp.dot(left, right, preferred_element_type=F32)


def dot_nt(left, right):
    return lax.dot_general(left, right, (((1,), (1,)), ((), ())), preferred_element_type=F32)


def dot_tn(left, right):
    return lax.dot_general(left, right, (((0,), (0,)), ((), ())), preferred_element_type=F32)


def iota(shape, dim):
    return lax.broadcasted_iota(I32, shape, dim)


def ones_where(mask):
    return jnp.where(mask, 1.0, 0.0).astype(BF16)


def low(index, count):
    return index & (count - 1)


def high(index, count):
    return lax.shift_right_logical(index, jnp.full(index.shape, count.bit_length() - 1, I32))


def sigmoid(value):
    return 1.0 / (1.0 + jnp.exp(-value))


def silu_slope(value):
    logistic = sigmoid(value)
    return logistic * (1.0 + value * (1.0 - logistic))


def rows(start, size):
    return pl.ds(pl.multiple_of(start, size), size)


def as_column(row):
    return jnp.transpose(jnp.broadcast_to(row, (LANES, LANES)))


def greet(nodes, grps):
    node, grp = lax.axis_index("node"), lax.axis_index("grp")
    barrier = pltpu.get_barrier_semaphore()

    def hello_node(step, _):
        peer = (lax.rem(node + step, nodes), grp)
        pl.semaphore_signal(barrier, inc=1, device_id=peer, device_id_type=MESH)
        return 0

    def hello_grp(step, _):
        peer = (node, lax.rem(grp + step, grps))
        pl.semaphore_signal(barrier, inc=1, device_id=peer, device_id_type=MESH)
        return 0

    lax.fori_loop(1, nodes, hello_node, 0)
    lax.fori_loop(1, grps, hello_grp, 0)
    return lambda: pl.semaphore_wait(barrier, nodes + grps - 2)


def offset(step, count):
    return lax.rem(jnp.where(lax.rem(step, 2) == 1, (step + 1) // 2, count - step // 2), count)


class Stage:
    def __init__(self, count, me, peer, source, landing, size, send_sem, recv_sem):
        self.count, self.me, self.peer, self.source = count, me, peer, source
        self.landing, self.size, self.send_sem, self.recv_sem = landing, size, send_sem, recv_sem

    def copy(self, to, place):
        return pltpu.make_async_remote_copy(
            src_ref=self.source(to),
            dst_ref=self.landing.at[rows(place * self.size, self.size), :],
            send_sem=self.send_sem.at[to],
            recv_sem=self.recv_sem.at[place],
            device_id=self.peer(to),
            device_id_type=MESH,
        )

    def each(self, act):
        def step(i, _):
            act(lax.rem(self.me + offset(i, self.count), self.count))
            return 0

        lax.fori_loop(1, self.count, step, 0)

    def start(self):
        self.each(lambda to: self.copy(to, self.me).start())

    def start_step(self, step):
        self.copy(lax.rem(self.me + offset(step, self.count), self.count), self.me).start()

    def arrive(self):
        self.each(lambda source: self.copy(source, source).wait_recv())

    def finish(self):
        self.each(lambda to: self.copy(to, self.me).wait_send())

    def total(self, own):
        def add(i, acc):
            source = lax.rem(self.me + i, self.count)
            return acc + self.landing[rows(source * self.size, self.size), :].astype(F32)

        return lax.fori_loop(1, self.count, add, own)


def to_pieces(value, ref):
    per = ref.shape[1] // LANES
    wide = value.shape[1] // LANES
    for k in range(value.shape[0] // 8 * wide):
        r, c = divmod(k, wide)
        piece, place = divmod(k, per)
        ref[piece * 8 : piece * 8 + 8, place * LANES : place * LANES + LANES] = value[
            r * 8 : r * 8 + 8, c * LANES : c * LANES + LANES
        ]


def from_pieces(ref, shape):
    per = ref.shape[1] // LANES
    wide = shape[1] // LANES
    bands = []
    for r in range(shape[0] // 8):
        band = []
        for c in range(wide):
            piece, place = divmod(r * wide + c, per)
            band.append(ref[piece * 8 : piece * 8 + 8, place * LANES : place * LANES + LANES])
        bands.append(jnp.concatenate(band, axis=1))
    return jnp.concatenate(bands, axis=0)


def start_together(stages):
    longest = max(stage.count for stage in stages)

    def turn(step, _):
        for stage in stages:
            if stage.count == longest:
                stage.start_step(step)
            else:
                pl.when(step < stage.count)(functools.partial(stage.start_step, step))
        return 0

    lax.fori_loop(1, longest, turn, 0)


class Path:
    def __init__(self, nodes, y_first, cap, refs, sems):
        node, self.grp = lax.axis_index("node"), lax.axis_index("grp")
        planes = nodes // ROW
        z, y = node // ROW, lax.rem(node, ROW)
        self.y_first = y_first
        self.firsts, self.seconds = (ROW, planes) if y_first else (planes, ROW)
        self.me1, self.me2 = (y, z) if y_first else (z, y)
        self.block = cap * self.seconds
        (self.tab, self.ws, self.es, self.wt, self.et, self.a, self.at, self.pt, self.out, self.inn, self.sums, self.sent, self.land,
         self.agg, self.out2, self.in2, self.code) = refs
        block, me1, me2 = self.block, self.me1, self.me2
        firsts, seconds, peer1, peer2 = self.firsts, self.seconds, self.peer1, self.peer2

        def own_tab(to):
            return self.tab.at[rows(me2 * 16, 16), :]

        def own_agg(to):
            return self.agg.at[rows(me2 * LANES, LANES), :]

        self.tables = Stage(seconds, me2, peer2, own_tab, self.tab, 16, sems[0], sems[1])
        self.rows_out = Stage(firsts, me1, peer1, lambda to: self.out.at[rows(to * block, block), :], self.inn, block, sems[2], sems[3])
        self.sums_out = Stage(seconds, me2, peer2, lambda to: self.sent.at[rows(to * LANES, LANES), :], self.land, LANES, sems[4], sems[5])
        self.agg_out = Stage(seconds, me2, peer2, own_agg, self.agg, LANES, sems[6], sems[7])
        self.rows_back = Stage(firsts, me1, peer1, lambda to: self.out2.at[rows(to * block, block), :], self.in2, block, sems[8], sems[9])

    def node_of(self, first, second):
        return second * ROW + first if self.y_first else first * ROW + second

    def peer1(self, to):
        return (self.node_of(to, self.me2), self.grp)

    def peer2(self, to):
        return (self.node_of(self.me1, to), self.grp)

    def first(self, step):
        return lax.rem(self.me1 + offset(step, self.firsts), self.firsts)

    def put_tables(self, owners, weights):
        self.tab[rows(self.me2 * 16, 8), :] = owners
        self.tab[rows(self.me2 * 16 + 8, 8), :] = weights

    def key_column(self, first, upper, lower):
        sub, lane = iota((self.block, LANES), 0), iota((self.block, LANES), 1)
        pick = ones_where(lane == self.node_of(first, low(sub, self.seconds)))
        listed = dot_nt(pick, upper) * 2.0 + dot_nt(pick, lower)
        return jnp.sum(jnp.where(lane == high(sub, self.seconds), listed, 0.0), axis=1, keepdims=True)

    def key_row(self, first, upper, lower):
        sub, lane = iota((self.block, LANES), 0), iota((self.block, LANES), 1)
        pick = ones_where(lane == self.node_of(first, low(sub, self.seconds)))
        listed = dot_nt(upper, pick) * 2.0 + dot_nt(lower, pick)
        sub, lane = iota((LANES, self.block), 0), iota((LANES, self.block), 1)
        return jnp.sum(jnp.where(sub == high(lane, self.seconds), listed, 0.0), axis=0, keepdims=True)

    def serve(self, first, upper, lower, messages):
        key = self.key_column(first, upper, lower)
        pick = ones_where(key == iota((self.block, messages.shape[0]), 1).astype(F32))
        self.out[rows(first * self.block, self.block), :] = dot(pick, messages[...]).astype(BF16)

    def keep(self, out, inn):
        own = rows(self.me1 * self.block, self.block)
        inn[own, :] = out[own, :]

    def read_tables(self, above):
        sub = iota((LANES, LANES), 0)

        def read(second, _):
            hits = jnp.zeros((LANES, LANES), F32)
            weights = jnp.zeros((LANES, LANES), F32)
            for k in range(8):
                hit = self.tab[pl.ds(second * 16 + k, 1), :] == sub
                hits = hits + jnp.where(hit, 1.0, 0.0)
                weights = weights + jnp.where(hit, self.tab[pl.ds(second * 16 + 8 + k, 1), :].astype(F32), 0.0)
            earlier = dot(hits.astype(BF16), above)
            at = rows(second * LANES, LANES)
            self.wt[:, at] = weights
            self.et[:, at] = earlier
            self.ws[at, :] = jnp.transpose(weights).astype(BF16)
            self.es[at, :] = jnp.transpose(earlier).astype(BF16)
            return 0

        lax.fori_loop(0, self.seconds, read, 0)

    def weigh(self, first):
        owner = self.node_of(first, self.me2)
        spread = ones_where(iota((LANES, self.block), 0) == owner)
        weight, slot = dot(self.ws[...], spread), dot(self.es[...], spread)
        lane = iota((8, self.block), 1)
        for second in range(self.seconds):
            at = slice(second * LANES, second * LANES + LANES)
            code = jnp.where(low(lane, self.seconds) == second, high(lane, self.seconds), -1).astype(F32)[:1]
            self.a[first, at, :] = jnp.where(slot[at] == code, weight[at], 0.0).astype(BF16)

    def number(self):
        sub = iota((self.block, LANES), 0)
        for second in range(self.seconds):
            self.code[second] = jnp.where(low(sub, self.seconds) == second, high(sub, self.seconds), -1).astype(F32)

    def weigh_back(self, first):
        owner = self.node_of(first, self.me2)
        weight, slot = self.wt[pl.ds(owner, 1), :], self.et[pl.ds(owner, 1), :]
        for second in range(self.seconds):
            at = slice(second * LANES, second * LANES + LANES)
            self.at[first, :, at] = jnp.where(slot[:, at] == self.code[second], weight[:, at], 0.0).astype(BF16)

    def spread(self, first, upper, lower):
        key = self.key_row(first, upper, lower)
        self.pt[first] = ones_where(iota((self.pt.shape[1], self.block), 0).astype(F32) == key)

    def finish(self):
        for stage in (self.tables, self.rows_out, self.sums_out, self.agg_out, self.rows_back):
            stage.finish()


class NodeSum:
    def __init__(self, nodes, pieces, z_in, mine, y_in, full, sems):
        node, grp = lax.axis_index("node"), lax.axis_index("grp")
        planes = nodes // ROW
        self.z, self.y = node // ROW, lax.rem(node, ROW)
        z, y = self.z, self.y
        self.pieces, self.mine, self.y_in, self.full = pieces, mine, y_in, full

        def z_peer(to):
            return (to * ROW + y, grp)

        def y_peer(to):
            return (z * ROW + to, grp)

        self.first = Stage(planes, z, z_peer, lambda to: pieces.at[rows(to * 8, 8), :], z_in, 8, sems[0], sems[1])
        self.second = Stage(ROW, y, y_peer, lambda to: mine, y_in, 8, sems[2], sems[3])
        self.third = Stage(planes, z, z_peer, lambda to: full.at[rows(z * 8, 8), :], full, 8, sems[4], sems[5])

    def begin(self, value):
        if self.pieces.shape[0] * self.pieces.shape[1] > value.shape[0] * value.shape[1]:
            self.pieces[...] = jnp.zeros_like(self.pieces)
        to_pieces(value, self.pieces)
        self.first.start()

    def over_y(self):
        self.first.arrive()
        own = self.first.total(self.pieces[rows(self.z * 8, 8), :])
        self.mine[...] = own
        self.y_in[rows(self.y * 8, 8), :] = own
        self.second.start()

    def gather(self):
        self.second.arrive()
        total = self.y_in[:8, :]
        for k in range(1, ROW):
            total = total + self.y_in[k * 8 : k * 8 + 8, :]
        self.full[rows(self.z * 8, 8), :] = total
        self.third.start()

    def end(self):
        self.third.arrive()

    def finish(self):
        for stage in (self.first, self.second, self.third):
            stage.finish()


class Ring:
    def __init__(self, grps, all_ref, size, send_sem, recv_sem):
        node, me = lax.axis_index("node"), lax.axis_index("grp")
        self.node, self.me, self.all_ref, self.size = node, me, all_ref, size
        self.send_sem, self.recv_sem = send_sem, recv_sem
        self.chips, self.core, self.chip = grps // 2, lax.rem(me, 2), me // 2
        self.hops = self.chips // 2
        self.index, self.started = {}, []
        for side in (0, 1):
            for hop in range(1, self.hops + 1):
                for piece in (0, 1):
                    if hop < self.hops or piece == side:
                        self.index["link", side, hop, piece] = len(self.index)
        for key in list(self.index):
            self.index[("core",) + key[1:]] = len(self.index)
        for piece in (0, 1):
            self.index["core", 0, 0, piece] = len(self.index)

    def at_chip(self, steps):
        return lax.rem(self.chip + self.chips + steps, self.chips) * 2 + self.core

    def origin(self, side, hop):
        return self.at_chip(-hop if side == 0 else hop)

    def copy(self, key):
        kind, side, hop, piece = key
        origin = self.origin(side, hop - 1 if kind == "link" else hop)
        half = self.size // 2
        at = rows(origin * self.size + piece * half, half)
        to = self.at_chip(1 if side == 0 else -1) if kind == "link" else self.chip * 2 + 1 - self.core
        return pltpu.make_async_remote_copy(
            src_ref=self.all_ref.at[at, :],
            dst_ref=self.all_ref.at[at, :],
            send_sem=self.send_sem.at[self.index[key]],
            recv_sem=self.recv_sem.at[self.index[key]],
            device_id=(self.node, to),
            device_id_type=MESH,
        )

    def start(self, *key):
        if key in self.index:
            self.copy(key).start()
            self.started.append(key)

    def arrive(self, *key):
        if key in self.index:
            self.copy(key).wait_recv()

    def begin(self):
        for piece in (0, 1):
            for side in (0, 1):
                self.start("link", side, 1, piece ^ side)
        for piece in (0, 1):
            self.start("core", 0, 0, piece)

    def step(self, hop):
        for piece in (0, 1):
            for side in (0, 1):
                key = (side, hop, piece ^ side)
                self.arrive("link", *key)
                self.start("link", side, hop + 1, piece ^ side)
                if ("link", *key) in self.index:
                    self.start("core", *key)

    def other(self, hop):
        for side in (0, 1):
            for piece in (0, 1):
                if hop or side == 0:
                    self.arrive("core", side, hop, piece)

    def finish(self):
        for key in self.started:
            self.copy(key).wait_send()


def tower_kernel(
    nodes, grps, nbr_ref, tgt_ref, msgw_ref, combw_ref, gain_ref, served_ref, owners_ref, weight_ref, labels_ref, pos_ref,
    loss_ref, mfull, cfull,
    msg0_ref, msg1_ref, bf_ref, slope_ref, upper_ref, lower_ref, path0, path1, sems0, sems1,
    comb_in_ref, pre_ref,
    all_ref, query_ref, gains_ref, rt_ref, ct_ref, gct_ref, ring_send, ring_recv, stat_ref, stat_send, stat_recv,
    acc_ref,
    cpart_ref, cland_ref, cpart_send, cpart_recv, cpieces, cz_in, cmine, cy_in, c0, c1, c2, c3, c4, c5,
    mpart_ref, pair_ref, pair_send, pair_recv, mhalf_ref, mland_ref, mx_send, mx_recv,
    mpieces, mz_in, mmine, my_in, m0, m1, m2, m3, m4, m5,
):
    ready = greet(nodes, grps)
    node, me = lax.axis_index("node"), lax.axis_index("grp")
    feat, tgts, pins = msgw_ref.shape[0], tgt_ref.shape[0], nbr_ref.shape[0]
    half, group = feat // 2, tgts * grps
    lane = iota((LANES, LANES), 1)
    sub = iota((LANES, LANES), 0)
    cap = served_ref.shape[0]
    paths = [Path(nodes, True, cap, path0, sems0), Path(nodes, False, cap, path1, sems1)]
    longest = max(path.firsts for path in paths)
    halves = (msg0_ref, msg1_ref)

    def each_first(first, act):
        def turn(step, _):
            for which, path in enumerate(paths):
                if path.firsts == longest:
                    act(path, which, step)
                else:
                    pl.when(step < path.firsts)(functools.partial(act, path, which, step))
            return 0

        lax.fori_loop(first, longest, turn, 0)

    def message(tile, _):
        at = rows(tile * LANES, LANES)
        nbr = nbr_ref[at, :].astype(BF16)
        bf_ref[at, :] = nbr
        pre = dot(nbr, msgw_ref[...])
        slope_ref[at, :] = pre
        msg = (pre * sigmoid(pre)).astype(BF16)
        msg0_ref[at, :] = msg[:, :half]
        msg1_ref[at, :] = msg[:, half:]
        return 0

    lax.fori_loop(0, pins // LANES, message, 0)
    upper_ref[...] = jnp.zeros_like(upper_ref)
    lower_ref[...] = jnp.zeros_like(lower_ref)
    served = served_ref[...]
    upper_ref[:cap, : served.shape[1]] = (served // 2).astype(F32)
    lower_ref[:cap, : served.shape[1]] = (served % 2).astype(F32)
    upper, lower = upper_ref[...].astype(BF16), lower_ref[...].astype(BF16)
    for path in paths:
        path.put_tables(owners_ref[...], weight_ref[...])
    ready()
    for path in paths:
        path.tables.start()

    def serve(path, which, step):
        first = path.first(step)
        path.serve(first, upper, lower, halves[which])
        path.rows_out.copy(first, path.me1).start()

    each_first(1, serve)
    for path, messages in zip(paths, halves):
        path.serve(path.me1, upper, lower, messages)
        path.keep(path.out, path.inn)

    above = ones_where(sub < lane)
    for path in paths:
        path.tables.arrive()
        path.read_tables(above)
    each_first(0, lambda path, which, step: path.weigh(path.first(step)))
    for path in paths:
        path.sums[...] = dot(path.a[path.me1], path.inn[rows(path.me1 * path.block, path.block), :])
    own_path = paths[0]
    total = jnp.sum(own_path.ws[rows(own_path.me2 * LANES, LANES), :].astype(F32), axis=1, keepdims=True)
    tgt_bf = tgt_ref[...].astype(BF16)
    comb_in_ref[:, :feat] = tgt_bf
    pre_ref[...] = dot(tgt_bf, combw_ref[:feat, :])

    def collect(path, which, step):
        first = path.first(step)
        path.rows_out.copy(first, first).wait_recv()
        path.sums[...] += dot(path.a[first], path.inn[rows(first * path.block, path.block), :])

    each_first(1, collect)
    for path in paths:
        path.sent[...] = path.sums[...].astype(BF16)
    start_together([path.sums_out for path in paths])

    for path in paths:
        path.number()
    each_first(0, lambda path, which, step: path.weigh_back(path.first(step)))
    gain = gain_ref[...]
    gain_hi = gain.astype(BF16).astype(F32)
    gain_mid = (gain - gain_hi).astype(BF16).astype(F32)
    gain_lo = gain - gain_hi - gain_mid
    tasks = gain.shape[0]
    gain3 = jnp.concatenate(
        [gain_hi, gain_mid, gain_lo, jnp.zeros((LANES - 3 * tasks, feat), F32)], axis=0
    ).astype(BF16)

    task = lane % tasks

    def gains(block, _):
        label = as_column(labels_ref[pl.ds(block, 1), :])
        pick = ones_where((label == task) & (lane < 3 * tasks))
        gains_ref[rows(block * tgts, tgts), :] = dot(pick, gain3)
        return 0

    lax.fori_loop(0, grps, gains, 0)
    sums = []
    for path in paths:
        path.sums_out.arrive()
        sums.append(path.sums_out.total(path.sums[rows(path.me2 * LANES, LANES), :]))
    agg_bf = (jnp.concatenate(sums, axis=1) / total).astype(BF16)
    comb_in_ref[:, feat:] = agg_bf
    comb_pre = pre_ref[...] + dot(agg_bf, combw_ref[feat:, :])
    hidden = comb_pre * sigmoid(comb_pre)
    inv_norm = lax.rsqrt(jnp.mean(hidden * hidden, axis=1, keepdims=True) + eps)
    embed = (hidden * inv_norm).astype(BF16)

    own = rows(me * tgts, tgts)
    all_ref[own, :] = embed
    ring = Ring(grps, all_ref, tgts, ring_send, ring_recv)
    ring.begin()
    own_gain = gains_ref[own, :]
    own_query = (embed.astype(F32) * own_gain).astype(BF16)

    def score(block):
        at = rows(block * tgts, tgts)
        block_embed = all_ref[at, :]
        block_query = (block_embed.astype(F32) * gains_ref[at, :]).astype(BF16)
        query_ref[at, :] = block_query
        rt_ref[at, :] = dot_nt(block_embed, own_query) * (1.0 / feat)
        ct_ref[at, :] = dot_nt(all_ref[own, :], block_query) * (1.0 / feat)

    score(me)
    for hop in range(1, ring.hops + 1):
        ring.step(hop)
        ring.other(hop - 1)
        if hop < ring.hops:
            score(ring.origin(0, hop))
            score(ring.origin(1, hop))
        else:
            score(ring.origin(0, hop))
        for side in (0, 1) if hop > 1 else (0,):
            score(ring.origin(side, hop - 1) + 1 - 2 * ring.core)
    ring.other(ring.hops)
    score(ring.origin(0, ring.hops) + 1 - 2 * ring.core)

    scores = rt_ref[...]
    top = jnp.max(scores, axis=0, keepdims=True)
    terms = jnp.exp(scores - top)
    norm = jnp.sum(terms, axis=0, keepdims=True)
    own_stat = rows(me * 8, 8)
    stat_ref[own_stat, :] = jnp.concatenate(
        [jnp.broadcast_to(top, (4, LANES)), jnp.broadcast_to(norm, (4, LANES))], axis=0
    )
    stats = Stage(grps, me, lambda to: (node, to), lambda to: stat_ref.at[own_stat, :], stat_ref, 8, stat_send, stat_recv)
    stats.start()
    hit = jnp.where(iota((group, tgts), 0) == pos_ref[pl.ds(me, 1), :], 1.0, 0.0)
    picked = jnp.sum(scores * hit, axis=0, keepdims=True)
    loss_ref[...] = top + jnp.log(norm) - picked
    grad = ((terms * (1.0 / norm) - hit) * (1.0 / group / feat)).astype(BF16)
    query_grad = dot_tn(grad, all_ref[...])
    stats.arrive()

    place = sub + me * tgts

    def column(block, _):
        stat = stat_ref[rows(block * 8, 8), :]
        terms = jnp.exp(ct_ref[rows(block * tgts, tgts), :] - stat[0:1, :]) * (1.0 / stat[4:5, :])
        hit = jnp.where(place == pos_ref[pl.ds(block, 1), :], 1.0, 0.0)
        gct_ref[:, rows(block * tgts, tgts)] = ((terms - hit) * (1.0 / group / feat)).astype(BF16)
        return 0

    lax.fori_loop(0, grps, column, 0, unroll=4)
    column_grad = dot(gct_ref[...], query_ref[...])
    embed_grad = query_grad * own_gain + column_grad
    logistic = sigmoid(comb_pre)
    inner = jnp.sum(hidden * embed_grad, axis=1, keepdims=True)
    cube = inv_norm * inv_norm * inv_norm
    hidden_grad = inv_norm * embed_grad - hidden * (cube * inner / feat)
    slope = logistic * (1.0 + comb_pre * (1.0 - logistic))
    pre_grad = (slope * hidden_grad).astype(BF16)
    agg = dot_nt(pre_grad, combw_ref[feat:, :]) / total

    agg_bf = agg.astype(BF16)
    for which, path in enumerate(paths):
        path.agg[rows(path.me2 * LANES, LANES), :] = agg_bf[:, which * half : which * half + half]
    start_together([path.agg_out for path in paths])

    cols = feat // grps
    cpart_ref[:, : 2 * feat] = dot_tn(pre_grad, comb_in_ref[...]).astype(BF16)
    pick = ones_where(as_column(labels_ref[pl.ds(me, 1), :]) == lane)
    head = query_grad * embed.astype(F32)
    head_hi = head.astype(BF16)
    head_lo = (head - head_hi.astype(F32)).astype(BF16)
    cpart_ref[:, 2 * feat :] = (dot_tn(head_hi, pick) + dot_tn(head_lo, pick)).astype(BF16)
    comb_sum = Stage(
        grps, me, lambda to: (node, to), lambda to: cpart_ref.at[rows(to * cols, cols), :], cland_ref, cols, cpart_send, cpart_recv
    )
    early = min(5, grps)
    lax.fori_loop(1, early, lambda step, _: (comb_sum.start_step(step), 0)[1], 0)
    comb_full = NodeSum(nodes, cpieces, cz_in, cmine, cy_in, cfull, (c0, c1, c2, c3, c4, c5))
    msg_full = NodeSum(nodes, mpieces, mz_in, mmine, my_in, mfull, (m0, m1, m2, m3, m4, m5))

    each_first(0, lambda path, which, step: path.spread(path.first(step), upper, lower))

    for path in paths:
        path.agg_out.arrive()

    def give(path, which, step):
        first = path.first(step)
        path.out2[rows(first * path.block, path.block), :] = dot(path.at[first], path.agg[...]).astype(BF16)
        path.rows_back.copy(first, path.me1).start()
        index = step + (4 if which == 0 else 11)
        limit = min(grps, 12 if which == 0 else 16)

        @pl.when(index < limit)
        def _():
            comb_sum.start_step(index)

    each_first(1, give)

    def slopes(tile, _):
        at = rows(tile * LANES, LANES)
        slope_ref[at, :] = silu_slope(slope_ref[at, :])
        return 0

    lax.fori_loop(0, pins // LANES, slopes, 0)
    for which, path in enumerate(paths):
        kept = dot(path.at[path.me1], path.agg[...]).astype(BF16)
        acc_ref[:, which * half : which * half + half] = dot(path.pt[path.me1], kept)

    def take(path, which, step):
        first = path.first(step)
        path.rows_back.copy(first, first).wait_recv()
        acc_ref[:, which * half : which * half + half] += dot(
            path.pt[first], path.in2[rows(first * path.block, path.block), :]
        )

    each_first(1, take)

    msg_grad = (slope_ref[...] * acc_ref[...]).astype(BF16)
    part = dot_tn(msg_grad, bf_ref[...]).astype(BF16)
    for g in range(grps):
        first = (g % 2) * half + (g // 2) * cols
        mpart_ref[first : first + cols, :] = part[g * cols : g * cols + cols, :]
    core, chip = lax.rem(me, 2), me // 2
    pair = pltpu.make_async_remote_copy(
        src_ref=mpart_ref.at[rows((1 - core) * half, half), :],
        dst_ref=pair_ref,
        send_sem=pair_send,
        recv_sem=pair_recv,
        device_id=(node, chip * 2 + 1 - core),
        device_id_type=MESH,
    )
    pair.start()
    comb_sum.arrive()
    comb_full.begin(comb_sum.total(cpart_ref[rows(me * cols, cols), :].astype(F32)))
    pair.wait_recv()
    mhalf_ref[...] = (mpart_ref[rows(core * half, half), :].astype(F32) + pair_ref[...].astype(F32)).astype(BF16)
    over_x = Stage(
        grps // 2, chip, lambda to: (node, to * 2 + core), lambda to: mhalf_ref.at[rows(to * cols, cols), :], mland_ref, cols, mx_send, mx_recv
    )
    over_x.start()
    comb_full.over_y()
    over_x.arrive()
    msg_full.begin(over_x.total(mhalf_ref[rows(chip * cols, cols), :].astype(F32)))
    comb_full.gather()
    msg_full.over_y()
    msg_full.gather()
    for path in paths:
        path.finish()
    ring.finish()
    stats.finish()
    comb_sum.finish()
    comb_full.end()
    comb_full.finish()
    pair.wait_send()
    over_x.finish()
    msg_full.end()
    msg_full.finish()


def outputs_kernel(loss_in, mfull, cfull, loss_ref, gmsg_ref, gcomb_ref, ghead_ref):
    loss_ref[...] = loss_in[...]
    gmsg_ref[...] = from_pieces(mfull, gmsg_ref.shape)
    cols, both = gcomb_ref.shape
    value = from_pieces(cfull, (cols, both + LANES))
    gcomb_ref[...] = value[:, :both]
    head = value[:, both:]
    if cols < LANES:
        head = jnp.concatenate([head, jnp.zeros((LANES - cols, LANES), F32)], axis=0)
    ghead_ref[...] = jnp.transpose(head)[: ghead_ref.shape[0], : ghead_ref.shape[1]]


def body(
    nodes, grps, nbr_feats, tgt_feats, msg_weight, comb_weight, head_gain, owners, serve_rows, importance,
    labels, positives,
):
    pins, feat = nbr_feats.shape
    tgts, tasks = tgt_feats.shape[0], head_gain.shape[0]
    group, half = tgts * grps, feat // 2
    cols, planes, chips = feat // grps, nodes // ROW, grps // 2
    hops, cap = chips // 2, serve_rows.shape[2]
    links = 2 * max(2 * hops - 1, 0)
    wide = 2 * feat + LANES

    def vm(kind, *shape):
        return pltpu.VMEM(shape, kind)

    def dma(*shape):
        return pltpu.SemaphoreType.DMA(shape)

    def per_of(width):
        return -(-(cols // 8 * (width // LANES)) // planes) * LANES

    def sum_scratch(width):
        per = per_of(width)
        piece = [vm(F32, planes * 8, per), vm(F32, planes * 8, per), vm(F32, 8, per), vm(F32, ROW * 8, per)]
        return piece + [dma(planes), dma(planes), dma(ROW), dma(ROW), dma(planes), dma(planes)]

    def path_scratch(firsts, seconds):
        block, tall = cap * seconds, seconds * LANES
        return [
            vm(I32, seconds * 16, LANES), vm(BF16, tall, LANES), vm(BF16, tall, LANES), vm(F32, LANES, tall), vm(F32, LANES, tall),
            vm(BF16, firsts, tall, block), vm(BF16, firsts, block, tall), vm(BF16, firsts, pins, block),
            vm(BF16, firsts * block, half), vm(BF16, firsts * block, half),
            vm(F32, tall, half), vm(BF16, tall, half), vm(BF16, tall, half), vm(BF16, tall, half),
            vm(BF16, firsts * block, half), vm(BF16, firsts * block, half), vm(F32, seconds, block, LANES),
        ]

    def path_sems(firsts, seconds):
        counts = [seconds, firsts, seconds, seconds, firsts]
        return [dma(count) for count in counts for _ in range(2)]

    scratch = [
        vm(BF16, pins, half), vm(BF16, pins, half), vm(BF16, pins, feat), vm(F32, pins, feat), vm(F32, LANES, LANES), vm(F32, LANES, LANES),
        path_scratch(ROW, planes), path_scratch(planes, ROW), path_sems(ROW, planes), path_sems(planes, ROW),
        vm(BF16, tgts, 2 * feat), vm(F32, tgts, feat),
        vm(BF16, group, feat), vm(BF16, group, feat), vm(F32, group, feat), vm(F32, group, tgts), vm(F32, group, tgts), vm(BF16, tgts, group),
        dma(2 * links + 2), dma(2 * links + 2), vm(F32, grps * 8, LANES), dma(grps), dma(grps),
        vm(F32, pins, feat),
        vm(BF16, feat, wide), vm(BF16, feat, wide), dma(grps), dma(grps), *sum_scratch(wide),
        vm(BF16, feat, feat), vm(BF16, half, feat), pltpu.SemaphoreType.DMA, pltpu.SemaphoreType.DMA,
        vm(BF16, half, feat), vm(BF16, half, feat), dma(chips), dma(chips), *sum_scratch(feat),
    ]
    args = (
        nbr_feats, tgt_feats, msg_weight, comb_weight, head_gain, serve_rows[0].T, owners.T, importance.T,
        labels.reshape(grps, tgts), positives.reshape(grps, tgts),
    )
    whole = pl.BlockSpec(memory_space=pltpu.VMEM)
    outs = [(1, tgts), (planes * 8, per_of(feat)), (planes * 8, per_of(wide))]
    sums = pl.pallas_call(
        functools.partial(tower_kernel, nodes, grps),
        name="tower",
        out_shape=[jax.ShapeDtypeStruct(shape, F32) for shape in outs],
        in_specs=[whole] * len(args),
        out_specs=[whole] * len(outs),
        scratch_shapes=scratch,
        compiler_params=pltpu.CompilerParams(
            collective_id=0, has_side_effects=True, vmem_limit_bytes=60 * 2**20
        ),
    )(*args)
    outs = [(1, tgts), (cols, feat), (cols, 2 * feat), (tasks, cols)]
    loss, grad_msg, grad_comb, grad_head = pl.pallas_call(
        outputs_kernel,
        name="outputs",
        out_shape=[jax.ShapeDtypeStruct(shape, F32) for shape in outs],
        in_specs=[whole] * len(sums),
        out_specs=[whole] * len(outs),
    )(*sums)
    return loss.reshape(tgts), grad_msg.T, grad_comb.T, grad_head


def solution(mesh):
    placed = (
        P(("node", "grp"), None),
        P(("node", "grp"), None),
        P(),
        P(),
        P(),
        P(("node", "grp"), None),
        P(("node", "grp"), None, None),
        P(("node", "grp"), None),
        P("node"),
        P("node"),
    )
    return jax.shard_map(
        functools.partial(body, mesh.shape["node"], mesh.shape["grp"]),
        mesh=mesh,
        in_specs=placed,
        out_specs=(P(("node", "grp")), P(None, "grp"), P(None, "grp"), P(None, "grp")),
        check_vma=False,
    )
```
